32 devices in a mesh: section: 2 (over y), dp: 8 (over z, x), tensor: 2 (over core).
Axes of the slice: x: 2, y: 2, z: 4, core: 2. Of those that a mesh axis runs over, the one named last changes fastest.
Arguments:
- layer_in: bfloat16 [2, 8, 256, 2048], P(None, 'dp', 'tensor', 'section'), may hold values from -6 to 6
- out_grad: bfloat16 [2, 8, 256, 2048], P(None, 'dp', 'tensor', 'section'), may hold values from -6 to 6
- doc_lengths: int32 [2, 8, 4], P(None, 'dp'), may hold values from 1 to 192, 256 in all within a row
- attn_gain: float32 [2, 2048], P('section'), may hold values from 0.1 to 1.9
- w_query: bfloat16 [2, 2048, 2048], P('section', 'dp', 'tensor'), may hold values from -0.125 to 0.125
- keyval_weight: bfloat16 [2, 2048, 2, 256], P('section', 'dp', None, 'tensor'), may hold values from -0.125 to 0.125
- w_out: bfloat16 [2, 2048, 2048], P('section', 'dp', 'tensor'), may hold values from -0.75 to 0.75
- mlp_gain: float32 [2, 2048], P('section'), may hold values from 0.1 to 1.9
- w_gate_up: bfloat16 [2, 2048, 2, 5632], P('section', 'dp', None, 'tensor'), may hold values from -0.125 to 0.125
- w_down: bfloat16 [2, 2048, 5632], P('section', 'dp', 'tensor'), may hold values from -0.078125 to 0.078125
Outputs:
- layer_out: bfloat16 [2, 8, 256, 2048], P(None, 'dp', 'tensor', 'section')
- in_grad: bfloat16 [2, 8, 256, 2048], P(None, 'dp', 'tensor', 'section')
- attn_gain_grad: float32 [2, 2048], P('section')
- w_query_grad: float32 [2, 2048, 2048], P('section', 'dp', 'tensor')
- w_keyval_grad: float32 [2, 2048, 2, 256], P('section', 'dp', None, 'tensor')
- w_out_grad: float32 [2, 2048, 2048], P('section', 'dp', 'tensor')
- mlp_gain_grad: float32 [2, 2048], P('section')
- w_gate_up_grad: float32 [2, 2048, 2, 5632], P('section', 'dp', None, 'tensor')
- w_down_grad: float32 [2, 2048, 5632], P('section', 'dp', 'tensor')
The draws below stay inside these ranges and needn't reach their ends.
Inputs may be any that keep to these rules, and one draw needn't show every extreme that they name: `doc_lengths`: each sequence's 4 lengths sum to 256; its longest document has 192 tokens.
All inputs are finite; a program needn't handle non-finite values.
Results may differ from the reference program's by a relative error of at most 0.035.
Values may be sent and summed in bfloat16 or wider, within the bound.
A program may use at most 384 MiB of HBM per device.

```python
import math
import jax
import jax.numpy as jnp
import numpy as np
from jax import lax

MODEL_WIDTH = 2048
QUERY_HEADS = 32
KEY_VALUE_HEADS = 4
HEAD_SIZE = 64
FF = 5632
LEN = 256
MB = 2
DOCS = 4
SEQS = 8
N_SECTION = 2


def levels(own_key, shape, split, least, high):
    loudness, own = 1.0, jax.random.fold_in(own_key, 6)
    for dim, parts in split:
        heights = jnp.exp(jax.random.uniform(jax.random.fold_in(own, dim), (parts,), jnp.float32, least / len(split), high / len(split)))
        loudness = loudness * jnp.repeat(heights, shape[dim] // parts).reshape([-1 if axis == dim else 1 for axis in range(len(shape))])
    return loudness


def profile(count, total, most, skew):
    portions = [(1 << 20) // math.isqrt(grade ** skew) + 1 for grade in range(2, count + 1)]
    surplus, given = total - most - (count - 1), [1] * (count - 1)
    while surplus > 0:
        candidates = [i for i in range(count - 1) if given[i] < most]
        mass, remaining = sum([portions[i] for i in candidates]), surplus
        for i in candidates:
            more = min(most - given[i], max(1, remaining * portions[i] // mass), surplus)
            given[i] = given[i] + more
            surplus = surplus - more
    return np.array([most] + given)


def ragged(own_key, number_of, total, limit, lean):
    if number_of == 2:
        one = jax.random.randint(own_key, (), max(1, total - limit), min(limit, total - 1) + 1)
        return jnp.stack([one, total - one])
    tallies = jnp.asarray(profile(number_of, total, limit, lean), jnp.int32)
    couples = (number_of - 1) // 2
    giver, receiver = tallies[1:1 + 2 * couples:2], tallies[2:2 + 2 * couples:2]
    slack = jnp.minimum(giver - 1, limit - receiver)
    moved = jax.random.randint(jax.random.fold_in(own_key, 1), (couples,), 0, 1 << 20) % (slack + 1)
    tallies = tallies.at[1:1 + 2 * couples:2].set(giver - moved).at[2:2 + 2 * couples:2].set(receiver + moved)
    return tallies[jax.random.permutation(jax.random.fold_in(own_key, 2), number_of)]


def centred(key, extent, spread, most, split=(), kind=jnp.bfloat16):
    gain = levels(key, extent, split, -0.22, 0.18) if split else 1.0
    array = jax.random.normal(key, extent, jnp.float32) * spread * gain
    return jnp.minimum(jnp.maximum(array, -most), most).astype(kind)


def setup_inputs(seed: int = 0) -> dict:
    arg_keys = jax.random.split(jax.random.key(seed), 11)
    layer_in = centred(arg_keys[0], (MB, SEQS, LEN, MODEL_WIDTH), 1.0, 6.0, ((1, 8), (2, 2), (3, 2)))
    out_grad = centred(arg_keys[1], (MB, SEQS, LEN, MODEL_WIDTH), 1.0, 6.0, ((1, 8), (2, 2), (3, 2)))
    doc_lengths = jax.vmap(lambda own: ragged(own, DOCS, LEN, LEN // 2 + LEN // 4, 1))(jax.random.split(arg_keys[2], MB * SEQS)).reshape((MB, SEQS, DOCS)).astype(jnp.int32)
    attn_gain = jnp.clip(1.0 + 0.18 * jax.random.normal(arg_keys[3], (N_SECTION, MODEL_WIDTH), jnp.float32), 0.1, 1.9)
    w_query = centred(arg_keys[4], (N_SECTION, MODEL_WIDTH, QUERY_HEADS * HEAD_SIZE), MODEL_WIDTH ** -0.5, 0.125, ((0, 2), (1, 8), (2, 2)))
    keyval_weight = centred(arg_keys[5], (N_SECTION, MODEL_WIDTH, 2, KEY_VALUE_HEADS * HEAD_SIZE), MODEL_WIDTH ** -0.5, 0.125, ((0, 2), (1, 8), (3, 2)))
    w_out = centred(arg_keys[6], (N_SECTION, MODEL_WIDTH, QUERY_HEADS * HEAD_SIZE), (QUERY_HEADS * HEAD_SIZE // 32) ** -0.5, 0.75, ((0, 2), (1, 8), (2, 2)))
    mlp_gain = jnp.clip(1.0 + 0.18 * jax.random.normal(arg_keys[7], (N_SECTION, MODEL_WIDTH), jnp.float32), 0.1, 1.9)
    w_gate_up = centred(arg_keys[8], (N_SECTION, MODEL_WIDTH, 2, FF), MODEL_WIDTH ** -0.5, 0.125, ((0, 2), (1, 8), (3, 2)))
    w_down = centred(arg_keys[9], (N_SECTION, MODEL_WIDTH, FF), FF ** -0.5, 0.078125, ((0, 2), (1, 8), (2, 2)))
    return {"layer_in": layer_in, "out_grad": out_grad, "doc_lengths": doc_lengths, "attn_gain": attn_gain, "w_query": w_query, "keyval_weight": keyval_weight, "w_out": w_out, "mlp_gain": mlp_gain, "w_gate_up": w_gate_up, "w_down": w_down}


NORM_EPSILON = 1e-05
ROPE_BASE = 10000.0
MASK_FILL = -1e+30
HIGHEST_PRECISION = lax.Precision.HIGHEST

@jax.custom_vjp
def lower_half(v):
    return lax.optimization_barrier(v.astype(jnp.bfloat16)).astype(jnp.float32)

@jax.custom_vjp
def low_back(v):
    return v

def low_keep(v):
    return (lower_half(v), None)

def low_pass(kept, grad):
    return (grad,)

def back_keep(v):
    return (v, None)

def back_low(kept, grad):
    return (lower_half(grad),)
lower_half.defvjp(low_keep, low_pass)
low_back.defvjp(back_keep, back_low)

def rope_tables(token_length, head_width):
    middle_col = head_width // 2
    frequency = ROPE_BASE ** (-(jnp.arange(middle_col, dtype=jnp.float32) * 2.0) / head_width)
    angles = jnp.arange(token_length, dtype=jnp.float32)[:, None] * frequency[None, :]
    cosine_table = jnp.concatenate([jnp.cos(angles), jnp.cos(angles)], 1)
    sine_values = jnp.concatenate([jnp.sin(angles), jnp.sin(angles)], 1)
    return (cosine_table, sine_values)

def rotate_halves(values, cosine_table, sine_values):
    middle_col = values.shape[-1] // 2
    turned = jnp.concatenate([-values[..., middle_col:], values[..., :middle_col]], -1)
    return values * cosine_table[:, None, :] + turned * sine_values[:, None, :]

def doc_mask(lengths, token_length):
    bounds = jnp.cumsum(lengths).astype(jnp.int32)
    places = jnp.arange(token_length, dtype=jnp.int32)
    owners = lax.optimization_barrier(jnp.sum((places[:, None] >= bounds[None, :]).astype(jnp.int32), 1))
    return (owners[:, None] == owners[None, :]) & (places[None, :] <= places[:, None])

def norm_rows(values, gain_row):
    inverse = lax.rsqrt(lax.optimization_barrier(jnp.mean(values * values, -1, keepdims=True)) + NORM_EPSILON)
    return values * inverse * gain_row

def layer(entering, params, visible, cosine_table, sine_values):
    attn_gain, w_query, keyval_weight, w_out, mlp_gain, w_gate_up, w_down = params
    token_length = entering.shape[0]
    query_groups = QUERY_HEADS // KEY_VALUE_HEADS
    normed = lower_half(norm_rows(entering, attn_gain))
    query_linear = low_back(jnp.dot(normed, w_query, precision=HIGHEST_PRECISION))
    keyval_linear = low_back(jnp.einsum('td,dkc->tkc', normed, keyval_weight, precision=HIGHEST_PRECISION))
    rotated_queries = lower_half(rotate_halves(query_linear.reshape(token_length, QUERY_HEADS, HEAD_SIZE), cosine_table, sine_values)).reshape(token_length, KEY_VALUE_HEADS, query_groups, HEAD_SIZE)
    rotated_keys = lower_half(rotate_halves(keyval_linear[:, 0].reshape(token_length, KEY_VALUE_HEADS, HEAD_SIZE), cosine_table, sine_values))
    value_lower_half = lower_half(keyval_linear[:, 1].reshape(token_length, KEY_VALUE_HEADS, HEAD_SIZE))
    scores = low_back(jnp.einsum('lhgc,mhc->hglm', rotated_queries, rotated_keys, precision=HIGHEST_PRECISION)) * HEAD_SIZE ** (-0.5)
    softmax_rows = jax.nn.softmax(jnp.where(visible, scores, MASK_FILL), axis=-1)
    attended = jnp.einsum('hglm,mhc->lhgc', lower_half(softmax_rows), value_lower_half, precision=HIGHEST_PRECISION).reshape(token_length, QUERY_HEADS * HEAD_SIZE)
    att_low = lower_half(low_back(attended))
    middle = entering + low_back(jnp.dot(att_low, w_out.T, precision=HIGHEST_PRECISION))
    normed_mlp = lower_half(norm_rows(middle, mlp_gain))
    gate_up = low_back(jnp.einsum('td,dkf->tkf', normed_mlp, w_gate_up, precision=HIGHEST_PRECISION))
    hidden = lower_half(low_back(jax.nn.silu(gate_up[:, 0]) * gate_up[:, 1]))
    return middle + low_back(jnp.dot(hidden, w_down.T, precision=HIGHEST_PRECISION))

def reference(layer_in, out_grad, doc_lengths, attn_gain, w_query, keyval_weight, w_out, mlp_gain, w_gate_up, w_down):
    params = tuple((member.astype(jnp.float32) for member in (attn_gain, w_query, keyval_weight, w_out, mlp_gain, w_gate_up, w_down)))
    cosine_table, sine_values = rope_tables(LEN, HEAD_SIZE)
    sequence_count = MB * SEQS
    inputs = layer_in.astype(jnp.float32).reshape(sequence_count, LEN, MODEL_WIDTH)
    cotangents = out_grad.astype(jnp.float32).reshape(sequence_count, LEN, MODEL_WIDTH)
    lengths = doc_lengths.reshape(sequence_count, DOCS)

    def one_sequence(running, sequence):
        entering, cotangent, bounds = sequence
        visible = doc_mask(bounds, LEN)

        def both_sections(values, weights):
            section_zero = tuple((member[0] for member in weights))
            section_one = tuple((member[1] for member in weights))
            handed = lower_half(low_back(layer(values, section_zero, visible, cosine_table, sine_values)))
            return layer(handed, section_one, visible, cosine_table, sine_values)
        leaving, pullback = jax.vjp(both_sections, entering, params)
        grad_entering, gradients = pullback(cotangent)
        running = jax.tree.map(lambda left_part, right_part: left_part + right_part, running, gradients)
        return (running, (leaving.astype(jnp.bfloat16), grad_entering.astype(jnp.bfloat16)))
    initial = jax.tree.map(jnp.zeros_like, params)
    gradients, (leavings, grad_inputs) = lax.scan(one_sequence, initial, (inputs, cotangents, lengths))
    layer_out = leavings.reshape(MB, SEQS, LEN, MODEL_WIDTH)
    in_grad = grad_inputs.reshape(MB, SEQS, LEN, MODEL_WIDTH)
    return (layer_out, in_grad, gradients[0], gradients[1], gradients[2], gradients[3], gradients[4], gradients[5], gradients[6])
```

```python
import functools

import jax
import jax.numpy as jnp
from jax import lax
from jax.experimental import pallas as pl
from jax.experimental.pallas import tpu as pltpu
from jax.sharding import PartitionSpec as P

HEAD_SIZE = 64
NORM_EPSILON = 1e-05
ROPE_BASE = 10000.0
MASK_FILL = -1e30
FACTOR = HEAD_SIZE ** (-0.5)
BF16 = jnp.bfloat16
F32 = jnp.float32

TENSOR = ("tensor", 0)
SECTION = ("section", 0)
SHARED = ("dp", 1)


def swap(block, place):
    axis, bit = place
    count = lax.axis_size(axis)
    return lax.ppermute(block, axis, [(i, i ^ (1 << bit)) for i in range(count)])


def side(place):
    axis, bit = place
    return (lax.axis_index(axis) >> bit) & 1


def pair(own, other, place, axis=0):
    first = side(place) == 0
    low = jnp.where(first, own, other)
    high = jnp.where(first, other, own)
    return jnp.stack([low, high], axis)


def pick(halves, which, axis):
    return lax.dynamic_index_in_dim(halves, which, axis, keepdims=False)


def dp_bits():
    count = lax.axis_size("dp")
    return [("dp", bit) for bit in reversed(range(count.bit_length() - 1))]


def rope_tables(token_length):
    middle = HEAD_SIZE // 2
    frequency = ROPE_BASE ** (-(jnp.arange(middle, dtype=F32) * 2.0) / HEAD_SIZE)
    angles = frequency[:, None] * jnp.arange(token_length, dtype=F32)[None, :]
    return (
        jnp.concatenate([jnp.cos(angles), jnp.cos(angles)], 0),
        jnp.concatenate([jnp.sin(angles), jnp.sin(angles)], 0),
    )


def owners_of(lengths, token_length):
    bounds = jnp.cumsum(lengths, -1)
    places = jnp.arange(token_length, dtype=jnp.int32)
    return jnp.sum((places[None, :, None] >= bounds[:, None, :]).astype(jnp.int32), -1)


def visible_block(owner_col, owner_row):
    length = owner_col.shape[0]
    key_place = lax.broadcasted_iota(jnp.int32, (length, length), 0)
    query_place = lax.broadcasted_iota(jnp.int32, (length, length), 1)
    return (owner_col == owner_row) & (key_place <= query_place)


def rope(u, cosine, sine):
    half = HEAD_SIZE // 2
    return u * cosine + jnp.concatenate([-u[half:], u[:half]], 0) * sine


def rope_back(u, cosine, sine):
    half = HEAD_SIZE // 2
    w = u * sine
    return u * cosine + jnp.concatenate([w[half:], -w[:half]], 0)


def attention_kernel(heads, qkv, cosine, sine, owner_col, owner_row, rotated, attended, log_total):
    cos, sin = cosine[...], sine[...]
    width = heads * HEAD_SIZE
    visible = visible_block(owner_col[0], owner_row[0])
    keys = rope(qkv[width : width + HEAD_SIZE, :], cos, sin).astype(BF16)
    values = qkv[width + HEAD_SIZE :, :].astype(BF16)
    rotated[width : width + HEAD_SIZE, :] = keys
    rotated[width + HEAD_SIZE :, :] = values
    for h in range(heads):
        at = slice(h * HEAD_SIZE, (h + 1) * HEAD_SIZE)
        queries = rope(qkv[at, :], cos, sin).astype(BF16)
        rotated[at, :] = queries
        score = lax.dot_general(keys, queries, (((0,), (0,)), ((), ())), preferred_element_type=F32)
        score = jnp.where(visible, score * FACTOR, MASK_FILL)
        top = jnp.max(score, 0, keepdims=True)
        exponent = jnp.exp(score - top)
        total = jnp.sum(exponent, 0, keepdims=True)
        prob = (exponent * (1.0 / total)).astype(BF16)
        attended[at, :] = jnp.dot(values, prob, preferred_element_type=F32).astype(BF16)
        log_total[0, h : h + 1, :] = top + jnp.log(total)


def attention_back_kernel(
    heads, rotated, grad_att, log_total, cosine, sine, owner_col, owner_row, grad_qkv
):
    cos, sin = cosine[...], sine[...]
    width = heads * HEAD_SIZE
    visible = visible_block(owner_col[0], owner_row[0])
    keys = rotated[width : width + HEAD_SIZE, :]
    values = rotated[width + HEAD_SIZE :, :]
    length = keys.shape[1]
    grad_keys = jnp.zeros((HEAD_SIZE, length), F32)
    grad_values = jnp.zeros((HEAD_SIZE, length), F32)
    for h in range(heads):
        at = slice(h * HEAD_SIZE, (h + 1) * HEAD_SIZE)
        queries = rotated[at, :]
        grad = grad_att[at, :]
        score = lax.dot_general(keys, queries, (((0,), (0,)), ((), ())), preferred_element_type=F32)
        score = jnp.where(visible, score * FACTOR, MASK_FILL)
        prob = jnp.exp(score - log_total[0, h : h + 1, :])
        grad_prob = lax.dot_general(
            values, grad, (((0,), (0,)), ((), ())), preferred_element_type=F32
        )
        inner = jnp.sum(prob * grad_prob, 0, keepdims=True)
        grad_score = (FACTOR * prob * (grad_prob - inner)).astype(BF16)
        grad_query = jnp.dot(keys, grad_score, preferred_element_type=F32)
        grad_qkv[at, :] = rope_back(grad_query, cos, sin).astype(BF16)
        grad_keys += lax.dot_general(
            queries, grad_score, (((1,), (1,)), ((), ())), preferred_element_type=F32
        )
        grad_values += lax.dot_general(
            grad, prob.astype(BF16), (((1,), (1,)), ((), ())), preferred_element_type=F32
        )
    grad_qkv[width : width + HEAD_SIZE, :] = rope_back(grad_keys, cos, sin).astype(BF16)
    grad_qkv[width + HEAD_SIZE :, :] = grad_values.astype(BF16)


def attention_specs(heads, length):
    rows = (heads + 2) * HEAD_SIZE
    whole = lambda height: pl.BlockSpec((height, length), lambda i: (0, i))
    table = pl.BlockSpec((HEAD_SIZE, length), lambda i: (0, 0))
    logs = pl.BlockSpec((1, heads, length), lambda i: (i, 0, 0))
    col = pl.BlockSpec((1, length, 1), lambda i: (i, 0, 0))
    row = pl.BlockSpec((1, 1, length), lambda i: (i, 0, 0))
    return whole(rows), whole(heads * HEAD_SIZE), logs, table, col, row


def attention(qkv, owners, tables):
    count, length = owners.shape
    heads = qkv.shape[0] // HEAD_SIZE - 2
    all_spec, head_spec, logs, table, col, row = attention_specs(heads, length)
    return pl.pallas_call(
        functools.partial(attention_kernel, heads),
        grid=(count,),
        out_shape=(
            jax.ShapeDtypeStruct(qkv.shape, BF16),
            jax.ShapeDtypeStruct((heads * HEAD_SIZE, qkv.shape[1]), BF16),
            jax.ShapeDtypeStruct((count, heads, length), F32),
        ),
        in_specs=[all_spec, table, table, col, row],
        out_specs=(all_spec, head_spec, logs),
        compiler_params=pltpu.CompilerParams(vmem_limit_bytes=32 * 1024 * 1024),
    )(qkv, *tables, owners[:, :, None], owners[:, None, :])


def attention_back(rotated, grad_att, log_total, owners, tables):
    count, length = owners.shape
    heads = rotated.shape[0] // HEAD_SIZE - 2
    all_spec, head_spec, logs, table, col, row = attention_specs(heads, length)
    return pl.pallas_call(
        functools.partial(attention_back_kernel, heads),
        grid=(count,),
        out_shape=jax.ShapeDtypeStruct(rotated.shape, BF16),
        in_specs=[all_spec, head_spec, logs, table, table, col, row],
        out_specs=all_spec,
        compiler_params=pltpu.CompilerParams(vmem_limit_bytes=32 * 1024 * 1024),
    )(rotated, grad_att, log_total, *tables, owners[:, :, None], owners[:, None, :])


def contract(left, right, left_dim, right_dim, kind=F32):
    return lax.dot_general(
        left, right, (((left_dim,), (right_dim,)), ((), ())), preferred_element_type=F32
    ).astype(kind)


def normed(values, gain):
    inverse = lax.rsqrt(jnp.mean(values * values, -1, keepdims=True) + NORM_EPSILON)
    return (values * inverse * gain).astype(BF16)


def norm_back(grad, values, gain):
    inverse = lax.rsqrt(jnp.mean(values * values, -1, keepdims=True) + NORM_EPSILON)
    scaled = values * inverse
    gained = grad * gain
    into = inverse * (gained - scaled * jnp.mean(gained * scaled, -1, keepdims=True))
    return into, jnp.sum(grad * scaled, 0, keepdims=True)


def reordered(values):
    count = lax.axis_size("dp")
    width = values.shape[-1]
    parts = values.reshape(values.shape[:-1] + (count, width // count))
    axis = parts.ndim - 2
    for _, bit in dp_bits():
        low = [lax.slice_in_dim(parts, i ^ (1 << bit), (i ^ (1 << bit)) + 1, axis=axis) for i in range(count)]
        parts = jnp.where(side(("dp", bit)) == 1, jnp.concatenate(low, axis), parts)
    return parts.reshape(values.shape)


class Wires:
    def __init__(self, send, recv):
        self.send, self.recv, self.count, self.started = send, recv, 0, []
        self.index = {name: lax.axis_index(name) for name in ("section", "dp", "tensor")}

    def partner(self, place):
        axis, bit = place
        where = dict(self.index)
        low = lax.rem(where[axis] // (1 << bit), 2)
        where[axis] = where[axis] + (1 - 2 * low) * (1 << bit)
        return (where["section"], where["dp"], where["tensor"])

    def go(self, source, target, place):
        copy = pltpu.make_async_remote_copy(
            src_ref=source,
            dst_ref=target,
            send_sem=self.send.at[self.count],
            recv_sem=self.recv.at[self.count],
            device_id=self.partner(place),
            device_id_type=pl.DeviceIdType.MESH,
        )
        self.count += 1
        copy.start()
        self.started.append(copy)
        return copy

    def drain(self):
        for copy in self.started:
            copy.wait_send()


def crossed(values, group):
    count = values.shape[-1] // group
    return jnp.concatenate(
        [values[:, (g ^ 1) * group : ((g ^ 1) + 1) * group] for g in range(count)], 1
    )


def exchange_kernel(rs, ag, middle, n_in, n_out, group, *refs):
    refs = list(refs)
    take = lambda count: [refs.pop(0) for _ in range(count)]
    partial = take(1)[0] if rs else None
    ins = take(n_in)
    gathered = take(1)[0] if ag else None
    outs = take(n_out)
    send, recv, local = take(3)
    wires = Wires(send, recv)
    section, tensor = wires.index["section"], wires.index["tensor"]
    places = [TENSOR, SECTION] + ([SHARED] if 8 in (rs, ag) else [])
    barrier = pltpu.get_barrier_semaphore()
    for place in places:
        pl.semaphore_signal(
            barrier, inc=1, device_id=wires.partner(place), device_id_type=pl.DeviceIdType.MESH
        )
    pl.semaphore_wait(barrier, len(places))
    total = None
    if rs == 8:
        mine, core, out, from_y, from_z, part_y, part_z = take(7)
        half = mine.shape[1] // 2
        lo, hi = pl.ds(0, half), pl.ds(half, half)
        near, far = {}, {}
        for c in (3, 1, 2, 0):
            near[c] = pltpu.make_async_copy(partial.at[2 * c], mine.at[c], local.at[c])
            near[c].start()
            far[c] = wires.go(partial.at[2 * c + 1], core.at[c], TENSOR)

        def ready(c):
            near[c].wait()
            far[c].wait_recv()

        def added(c, rows):
            return mine[c, rows, :].astype(F32) + core[c, rows, :].astype(F32)

        ready(3)
        out[2, lo, :] = added(3, lo).astype(BF16)
        diag_y = wires.go(out.at[2, lo], part_y, SECTION)
        out[2, hi, :] = crossed(added(3, hi), group).astype(BF16)
        diag_z = wires.go(out.at[2, hi], part_z, SHARED)
        ready(1)
        out[0, lo, :] = added(1, lo).astype(BF16)
        first_y = wires.go(out.at[0, lo], from_y.at[lo], SECTION)
        ready(2)
        out[1, hi, :] = crossed(added(2, hi), group).astype(BF16)
        first_z = wires.go(out.at[1, hi], from_z.at[hi], SHARED)
        diag_y.wait_recv()
        out[1, lo, :] = crossed(added(2, lo) + part_y[...].astype(F32), group).astype(BF16)
        second_z = wires.go(out.at[1, lo], from_z.at[lo], SHARED)
        diag_z.wait_recv()
        out[0, hi, :] = (added(1, hi) + part_z[...].astype(F32)).astype(BF16)
        second_y = wires.go(out.at[0, hi], from_y.at[hi], SECTION)
        ready(0)
        for copy in (first_y, second_y, first_z, second_z):
            copy.wait_recv()
        total = (
            mine[0].astype(F32) + core[0].astype(F32) + from_y[...].astype(F32) + from_z[...].astype(F32)
        )
    elif rs == 4:
        mine, core, out, from_y = take(4)
        near, far = {}, {}
        for c in (1, 0):
            slot = 2 * (section + c - 2 * c * section)
            near[c] = pltpu.make_async_copy(partial.at[slot + tensor], mine.at[c], local.at[c])
            near[c].start()
            far[c] = wires.go(partial.at[slot + 1 - tensor], core.at[c], TENSOR)
        near[1].wait()
        far[1].wait_recv()
        out[...] = (mine[1].astype(F32) + core[1].astype(F32)).astype(BF16)
        over_y = wires.go(out, from_y, SECTION)
        near[0].wait()
        far[0].wait_recv()
        over_y.wait_recv()
        total = mine[0].astype(F32) + core[0].astype(F32) + from_y[...].astype(F32)
    rows = middle(total, ins, outs)
    if ag:
        own = take(1)[0]
        own[...] = rows
        half = own.shape[0] // 2
        lo, hi = pl.ds(0, half), pl.ds(half, half)
    if ag == 8:
        turned = take(1)[0]
        turned[...] = crossed(rows, group)
        over_y_hi = wires.go(own.at[hi], gathered.at[2, hi], SECTION)
        over_z_lo = wires.go(turned.at[lo], gathered.at[4, lo], SHARED)
        over_y_lo = wires.go(own.at[lo], gathered.at[2, lo], SECTION)
        over_z_hi = wires.go(turned.at[hi], gathered.at[4, hi], SHARED)
        over_core = [wires.go(own, gathered.at[1], TENSOR)]
        keep = pltpu.make_async_copy(own, gathered.at[0], local.at[4])
        keep.start()
        diag = []
        over_y_hi.wait_recv()
        for g in range(own.shape[1] // group):
            diag.append(
                wires.go(
                    gathered.at[2, hi, pl.ds(g * group, group)],
                    gathered.at[6, hi, pl.ds((g ^ 1) * group, group)],
                    SHARED,
                )
            )
        over_z_lo.wait_recv()
        diag.append(wires.go(gathered.at[4, lo], gathered.at[6, lo], SECTION))
        over_y_lo.wait_recv()
        over_core.append(wires.go(gathered.at[2], gathered.at[3], TENSOR))
        over_z_hi.wait_recv()
        over_core.append(wires.go(gathered.at[4], gathered.at[5], TENSOR))
        for copy in diag:
            copy.wait_recv()
        over_core.append(wires.go(gathered.at[6], gathered.at[7], TENSOR))
        for copy in over_core:
            copy.wait_recv()
        keep.wait()
    elif ag == 4:
        slot = 2 * section + tensor
        across = 2 * (1 - section) + tensor
        over_y = wires.go(own, gathered.at[slot], SECTION)
        over_core = [wires.go(own, gathered.at[slot], TENSOR)]
        keep = pltpu.make_async_copy(own, gathered.at[slot], local.at[4])
        keep.start()
        over_y.wait_recv()
        over_core.append(wires.go(gathered.at[across], gathered.at[across], TENSOR))
        for copy in over_core:
            copy.wait_recv()
        keep.wait()
    wires.drain()


def exchange(rs, ag, middle, partial, ins, outs, collective_id):
    rows, width = 0, 0
    if rs:
        rows, width = partial.shape[0] // rs, partial.shape[1]
        partial = partial.reshape(rs, rows, width)
    else:
        rows, width = ins[0].shape
    group = 2 * width // lax.axis_size("dp")
    block = lambda *lead: pltpu.VMEM(lead + (rows, width), BF16)
    anywhere = pl.BlockSpec(memory_space=pl.ANY)
    inside = pl.BlockSpec(memory_space=pltpu.VMEM)
    wires = 16 + 2 * (width // group)
    scratch = [
        pltpu.SemaphoreType.DMA((wires,)),
        pltpu.SemaphoreType.DMA((wires,)),
        pltpu.SemaphoreType.DMA((5,)),
    ]
    if rs == 8:
        part = pltpu.VMEM((rows // 2, width), BF16)
        scratch += [block(4), block(4), block(3), block(), block(), part, part]
    elif rs == 4:
        scratch += [block(2), block(2), block(), block()]
    if ag:
        scratch += [block()]
    if ag == 8:
        scratch += [block()]
    out_shape = ([jax.ShapeDtypeStruct((ag, rows, width), BF16)] if ag else []) + list(outs)
    results = pl.pallas_call(
        functools.partial(exchange_kernel, rs, ag, middle, len(ins), len(outs), group),
        out_shape=out_shape,
        in_specs=([anywhere] if rs else []) + [inside] * len(ins),
        out_specs=([anywhere] if ag else []) + [inside] * len(outs),
        scratch_shapes=scratch,
        compiler_params=pltpu.CompilerParams(
            collective_id=collective_id, has_side_effects=True, vmem_limit_bytes=40 * 1024 * 1024
        ),
    )(*(([partial] if rs else []) + list(ins)))
    results = list(results)
    if ag:
        results[0] = results[0].reshape(ag * rows, width)
    return results


def start_rows(total, ins, outs):
    return normed(ins[0][...], ins[1][...])


def bare_rows(total, ins, outs):
    return ins[0][...]


def forward_rows(total, ins, outs):
    middle = ins[0][...] + total
    outs[0][...] = middle
    return normed(middle, ins[1][...])


def handed_rows(total, ins, outs):
    handed = (ins[0][...] + total).astype(BF16).astype(F32)
    outs[0][...] = handed
    return normed(handed, ins[1][...])


def last_rows(total, ins, outs):
    outs[0][...] = (ins[0][...] + total).astype(BF16)


def back_rows(total, ins, outs):
    through, values, gain = ins
    into, term = norm_back(total, values[...], gain[...])
    result = through[...].astype(F32) + into
    outs[1][...] = term
    outs[0][...] = result.astype(outs[0].dtype)
    return result.astype(BF16)


def like(block, kind):
    return jax.ShapeDtypeStruct(block.shape, kind)


def mlp_forward(rows_mlp, weights):
    w_gu, w_d = weights[1:]
    gate_up = contract(rows_mlp, w_gu, 1, 0)
    units = gate_up.shape[1] // 2
    gate, up = gate_up[:, :units], gate_up[:, units:]
    hidden = (gate * jax.nn.sigmoid(gate) * up).astype(BF16)
    return gate_up, hidden, contract(hidden, w_d, 1, 1, BF16)


def mlp_backward(grad_out, rows_mlp, gate_up, hidden, weights):
    w_gu, w_d = weights[1:]
    term_d = contract(grad_out, hidden, 0, 0, BF16)
    grad_hidden = contract(grad_out, w_d, 1, 0, BF16).astype(F32)
    units = gate_up.shape[1] // 2
    gate, up = gate_up[:, :units], gate_up[:, units:]
    sig = jax.nn.sigmoid(gate)
    grad_gate = grad_hidden * up * sig * (1.0 + gate * (1.0 - sig))
    grad_up = grad_hidden * (gate * sig)
    grad_gu = jnp.concatenate([grad_gate, grad_up], 1).astype(BF16)
    partial = contract(grad_gu, w_gu, 1, 1, BF16)
    return partial, term_d, contract(rows_mlp, grad_gu, 0, 0, BF16)


def attn_forward(rows_attn, weights, owners, tables):
    w_attn = weights[0]
    width = w_attn.shape[1] - attn_split(w_attn)
    qkv = contract(w_attn[:, : attn_split(w_attn)], rows_attn, 0, 1)
    rotated, attended, log_total = attention(qkv, owners, tables)
    return rotated, attended, log_total, contract(attended, w_attn[:, attn_split(w_attn) :], 0, 1, BF16)


def attn_split(w_attn):
    return (w_attn.shape[1] - 2 * HEAD_SIZE) // 2 + 2 * HEAD_SIZE


def attn_backward(grad_branch, rows_attn, rotated, attended, log_total, weights, owners, tables):
    w_attn = weights[0]
    at = attn_split(w_attn)
    grad_att = contract(w_attn[:, at:], grad_branch, 0, 1, BF16)
    grad_qkv = attention_back(rotated, grad_att, log_total, owners, tables)
    partial = contract(grad_qkv, w_attn[:, :at], 0, 1, BF16)
    term_o = contract(grad_branch, attended, 0, 1, BF16)
    term_qkv = contract(rows_attn, grad_qkv, 0, 1, BF16)
    return partial, jnp.concatenate([term_qkv, term_o], 1)


X_BIT = ("dp", 0)


class Hops(Wires):
    def __init__(self, send, recv):
        super().__init__(send, recv)
        self.other = 1 - self.index["section"]

    def to(self, offset):
        dp = self.index["dp"]
        for bit in range(offset.bit_length()):
            if offset >> bit & 1:
                low = lax.rem(dp // (1 << bit), 2)
                dp = dp + (1 - 2 * low) * (1 << bit)
        return (self.index["section"], dp, self.index["tensor"])

    def across(self):
        return (self.other, self.index["dp"], self.index["tensor"])

    def make(self, source, target, device):
        copy = pltpu.make_async_remote_copy(
            src_ref=source,
            dst_ref=target,
            send_sem=self.send.at[self.count],
            recv_sem=self.recv.at[self.count],
            device_id=device,
            device_id_type=pl.DeviceIdType.MESH,
        )
        return copy

    def start(self, source, target, device):
        copy = self.make(source, target, device)
        self.count += 1
        copy.start()
        self.started.append(copy)
        return copy

    def start_either(self, choice, first, second, target, device):
        copy = self.make(first, target, device)
        backup = self.make(second, target, device)
        self.count += 1
        pl.when(choice)(copy.start)
        pl.when(jnp.logical_not(choice))(backup.start)
        self.started.append(copy)
        return copy

    def greet(self, offsets):
        barrier = pltpu.get_barrier_semaphore()
        devices = [self.to(offset) for offset in offsets] + [self.across()]
        for device in devices:
            pl.semaphore_signal(
                barrier, inc=1, device_id=device, device_id_type=pl.DeviceIdType.MESH
            )
        pl.semaphore_wait(barrier, len(devices))


def reached(count):
    return [1] + [2 * k for k in range(1, count // 2)]


def gather_kernel(count, *refs):
    packs, crossed_over, full = refs[:3], refs[3:6], (refs[6:9], refs[9:12])
    send, recv, local = refs[12:]
    hops = Hops(send, recv)
    section = hops.index["section"]
    half = lax.rem(hops.index["dp"] // 2, 2)
    kinds = count // 2
    hops.greet(reached(count))
    keeps = []
    over = [
        hops.start(packs[a].at[hops.other], crossed_over[a], hops.across()) for a in range(3)
    ]

    def source(a, layer, other):
        if a == 0:
            return packs[0].at[section], crossed_over[0]
        which = 1 - half if other else half
        return packs[a].at[section, which], crossed_over[a].at[which]

    def from_source(a, layer, other, target, device):
        first, second = source(a, layer, other)
        return hops.start_either(section == layer, first, second, target, device)

    arrived = {}

    def begin(a, layer):
        out = full[layer][a]
        first, second = source(a, layer, False)
        keep = pltpu.make_async_copy(first, out.at[0], local.at[3 * layer + a])
        backup = pltpu.make_async_copy(second, out.at[0], local.at[3 * layer + a])
        pl.when(section == layer)(keep.start)
        pl.when(section != layer)(backup.start)
        keeps.append(keep)
        for k in reversed(range(1, kinds)):
            if a > 0 or k == 1 or k % 2 == 0:
                arrived[a, layer, k] = from_source(
                    a, layer, k % 2 == 1, out.at[2 * k], hops.to(2 * k)
                )
        arrived[a, layer, "x0"] = from_source(a, layer, False, out.at[1], hops.to(1))

    def onward(a, layer):
        out = full[layer][a]
        for k in reversed(range(1, kinds)):
            if a > 0 or k == 1 or k % 2 == 0:
                arrived[a, layer, k].wait_recv()
                arrived[a, layer, "x", k] = hops.start(out.at[2 * k], out.at[2 * k + 1], hops.to(1))
                if a == 0 and k % 2 == 0:
                    arrived[a, layer, k + 1] = hops.start(
                        out.at[2 * k], out.at[2 * k + 2], hops.to(2)
                    )

    def finish(a, layer):
        out = full[layer][a]
        if a == 0:
            for k in reversed(range(2, kinds, 2)):
                arrived[a, layer, "x", k].wait_recv()
                arrived[a, layer, "x", k + 1] = hops.start(
                    out.at[2 * k + 1], out.at[2 * k + 3], hops.to(2)
                )

    order = [(0, 0), (1, 0), (2, 0), (0, 1), (1, 1), (2, 1)]
    for place, (a, layer) in enumerate(order):
        if layer == 0:
            over[a].wait_recv()
        begin(a, layer)
        if place:
            onward(*order[place - 1])
        if place > 1:
            finish(*order[place - 2])
    onward(*order[-1])
    finish(*order[-2])
    finish(*order[-1])
    for a, layer in order:
        arrived[a, layer, "x0"].wait_recv()
        for k in range(1, kinds):
            if a == 0 and k % 2 == 1 and k > 1:
                arrived[a, layer, k].wait_recv()
            if a > 0 or k % 2 == 1:
                arrived[a, layer, "x", k].wait_recv()
    for keep in keeps:
        keep.wait()
    hops.drain()


def gathered_weights(packs):
    count = lax.axis_size("dp")
    anywhere = pl.BlockSpec(memory_space=pl.ANY)
    rows = packs[0].shape[-2]
    over = [jax.ShapeDtypeStruct(pack.shape[1:], BF16) for pack in packs]
    full = [jax.ShapeDtypeStruct((count, rows, pack.shape[-1]), BF16) for pack in packs]
    wires = 3 + 6 * (count - 1)
    results = pl.pallas_call(
        functools.partial(gather_kernel, count),
        out_shape=over + full + full,
        in_specs=[anywhere] * 3,
        out_specs=[anywhere] * 9,
        scratch_shapes=[
            pltpu.SemaphoreType.DMA((wires,)),
            pltpu.SemaphoreType.DMA((wires,)),
            pltpu.SemaphoreType.DMA((6,)),
        ],
        compiler_params=pltpu.CompilerParams(collective_id=10, has_side_effects=True),
    )(*packs)
    flat = [block.reshape(-1, block.shape[-1]) for block in results[3:]]
    return flat[:3], flat[3:]


CHUNK = 32


def scatter_kernel(count, rows, *refs):
    terms, outs = (refs[:3], refs[3:6]), refs[6:9]
    send, recv, local = refs[9:12]
    landed, loaded = (refs[12:15], refs[15:18]), (refs[18:21], refs[21:24])
    distant = (refs[24:27], refs[27:30])
    hops = Hops(send, recv)
    section = hops.index["section"]
    half = lax.rem(hops.index["dp"] // 2, 2)
    kinds = count // 2
    hops.greet(reached(count))
    chunk = min(CHUNK, rows)

    def add(target, sources):
        @pl.loop(0, rows // chunk)
        def _(i):
            at = pl.ds(pl.multiple_of(i * chunk, chunk), chunk)
            total = sources[0][at, :].astype(F32)
            for source in sources[1:]:
                total = total + source[at, :].astype(F32)
            target[at, :] = total.astype(BF16)

    copies, loads = {}, {}
    used = [0]

    def load(a, layer, r):
        copy = pltpu.make_async_copy(
            terms[layer][a].at[r], loaded[layer][a].at[r // 2], local.at[used[0]]
        )
        used[0] += 1
        copy.start()
        return copy

    def begin(a, layer):
        term, land = terms[layer][a], landed[layer][a]
        for k in reversed(range(kinds)):
            if a > 0 or k < 2 or k % 2 == 0:
                loads[a, layer, k] = load(a, layer, 2 * k)
        if a == 0:
            for k in range(2, kinds, 2):
                for j in (1, 0):
                    copies[a, layer, "s", k + j] = hops.start(
                        term.at[2 * k + 2 + j], land.at[kinds + k + j], hops.to(2)
                    )
                copy = pltpu.make_async_copy(
                    term.at[2 * k + 1], loaded[layer][a].at[k + 1], local.at[used[0]]
                )
                used[0] += 1
                copy.start()
                loads[a, layer, "x", k] = copy
        for k in reversed(range(kinds)):
            if a > 0 or k < 2:
                copies[a, layer, "x", k] = hops.start(term.at[2 * k + 1], land.at[k], hops.to(1))

    def shared_first(a, layer):
        if a:
            return
        land, kept = landed[layer][a], loaded[layer][a]
        for k in range(2, kinds, 2):
            copies[a, layer, "s", k + 1].wait_recv()
            loads[a, layer, "x", k].wait()
            add(kept.at[k + 1], [kept.at[k + 1], land.at[kinds + k + 1]])
            copies[a, layer, "x", k] = hops.start(kept.at[k + 1], land.at[k], hops.to(1))

    def onward(a, layer):
        land, kept = landed[layer][a], loaded[layer][a]
        for k in reversed(range(kinds)):
            if a == 0 and k > 1 and k % 2 == 1:
                continue
            loads[a, layer, k].wait()
            copies[a, layer, "x", k].wait_recv()
            parts = [kept.at[k], land.at[k]]
            if a == 0 and k > 1:
                copies[a, layer, "s", k].wait_recv()
                parts.append(land.at[kinds + k])
            add(kept.at[k], parts)
            if k:
                copies[a, layer, "z", k] = hops.start(
                    kept.at[k], distant[layer][a].at[k - 1], hops.to(2 * k)
                )

    ending = []

    def finish(a, layer):
        kept, far = loaded[layer][a], distant[layer][a]
        result = landed[layer][a]
        mine, other = [kept.at[0]], []
        for k in range(1, kinds):
            if (a, layer, "z", k) in copies:
                copies[a, layer, "z", k].wait_recv()
                (other if a and k % 2 else mine).append(far.at[k - 1])
        if a:
            add(result.at[0], mine)
            add(result.at[1], other)
            pieces = [(result.at[0], half), (result.at[1], 1 - half)]
        else:
            add(result.at[0], mine)
            pieces = [(result.at[0], None)]
        for piece, which in pieces:
            target = outs[a].at[section] if which is None else outs[a].at[section, which]
            index = used[0]
            used[0] += 1
            keep = pltpu.make_async_copy(piece, target, local.at[index])
            away = hops.make(piece, target, hops.across())
            hops.count += 1
            pl.when(section == layer)(keep.start)
            pl.when(section != layer)(away.start)
            ending.append((layer, keep, away))

    order = [(2, 1), (1, 1), (0, 1), (2, 0), (1, 0), (0, 0)]
    for place, (a, layer) in enumerate(order):
        begin(a, layer)
        if place:
            onward(*order[place - 1])
        shared_first(a, layer)
        if place > 1:
            finish(*order[place - 2])
    onward(*order[-1])
    finish(*order[-2])
    finish(*order[-1])
    for layer, keep, away in ending:
        @pl.when(section == layer)
        def _():
            keep.wait()
            away.wait_recv()

        pl.when(section != layer)(away.wait_send)
    hops.drain()


def scattered_terms(terms, rows):
    count = lax.axis_size("dp")
    kinds = count // 2
    anywhere = pl.BlockSpec(memory_space=pl.ANY)
    flat = [term.reshape(count, rows, term.shape[1]) for term in terms[0] + terms[1]]
    columns = [term.shape[1] for term in terms[0]]
    outs = [
        jax.ShapeDtypeStruct((2, rows, columns[0]), BF16),
        jax.ShapeDtypeStruct((2, 2, rows, columns[1]), BF16),
        jax.ShapeDtypeStruct((2, 2, rows, columns[2]), BF16),
    ]
    wires = 12 + 6 * (count + kinds)
    block = lambda depth, a: pltpu.VMEM((depth, rows, columns[a]), BF16)
    landed = [block(2 * kinds if a == 0 else kinds, a) for a in range(3)]
    loaded = [block(kinds, a) for a in range(3)]
    distant = [block(kinds - 1, a) for a in range(3)]
    return pl.pallas_call(
        functools.partial(scatter_kernel, count, rows),
        out_shape=outs,
        in_specs=[anywhere] * 6,
        out_specs=[anywhere] * 3,
        scratch_shapes=[
            pltpu.SemaphoreType.DMA((wires,)),
            pltpu.SemaphoreType.DMA((wires,)),
            pltpu.SemaphoreType.DMA((wires,)),
        ]
        + landed
        + landed
        + loaded
        + loaded
        + distant
        + distant,
        compiler_params=pltpu.CompilerParams(
            collective_id=11, has_side_effects=True, vmem_limit_bytes=58 * 1024 * 1024
        ),
    )(*flat)


def halves(block, axis):
    shape = block.shape
    return block.reshape(shape[:axis] + (2, shape[axis] // 2) + shape[axis + 1 :])


def shards(
    layer_in,
    out_grad,
    doc_lengths,
    attn_gain,
    w_query,
    keyval_weight,
    w_out,
    mlp_gain,
    w_gate_up,
    w_down,
):
    section = lax.axis_index("section")
    first = section == 0
    micro, seqs, here, columns = layer_in.shape
    length = here * lax.axis_size("tensor")
    rows = w_query.shape[1]

    def whole_rows(block):
        kept = pick(block, section, 0)
        other = swap(pick(block, 1 - section, 0), SECTION)
        joined = pair(kept, other, SECTION, 2)
        return reordered(joined.reshape(seqs * here, 2 * columns))

    gain_block = jnp.concatenate([attn_gain, mlp_gain], 0)
    gains_both = reordered(pair(gain_block, swap(gain_block, SECTION), SECTION, 0))
    attn_gains = [gains_both[layer, 0][None] for layer in range(2)]
    mlp_gains = [gains_both[layer, 1][None] for layer in range(2)]
    entering = whole_rows(layer_in).astype(F32)
    cotangent = whole_rows(out_grad)

    q = halves(w_query[0], 1)
    kv = halves(keyval_weight[0], 2).swapaxes(1, 2).reshape(rows, 2, -1)
    pack_attn = jnp.concatenate([q, kv, halves(w_out[0], 1)], 2).swapaxes(0, 1)
    pack_gu = halves(halves(w_gate_up[0], 2), 3).transpose(2, 3, 0, 1, 4).reshape(2, 2, rows, -1)
    pack_d = halves(halves(w_down[0], 1), 2).transpose(1, 2, 0, 3)
    weights = gathered_weights([pack_attn, pack_gu, pack_d])
    owners = owners_of(doc_lengths.reshape(micro * seqs, -1), length)
    tables = rope_tables(length)
    gain_like = jax.ShapeDtypeStruct((1, entering.shape[1]), F32)

    entered, middles, saved = [], [], []
    (rows_attn,) = exchange(0, 4, start_rows, None, [entering, attn_gains[0]], [], 0)
    for layer in range(2):
        entered.append(entering)
        rotated, attended, log_total, partial = attn_forward(
            rows_attn, weights[layer], owners, tables
        )
        rows_mlp, middle = exchange(
            4,
            8,
            forward_rows,
            partial,
            [entering, mlp_gains[layer]],
            [like(entering, F32)],
            1 + 2 * layer,
        )
        middles.append(middle)
        gate_up, hidden, partial = mlp_forward(rows_mlp, weights[layer])
        saved.append((rows_attn, rotated, attended, log_total, rows_mlp, gate_up, hidden))
        if layer == 0:
            rows_attn, entering = exchange(
                8, 4, handed_rows, partial, [middle, attn_gains[1]], [like(entering, F32)], 2
            )
        else:
            (last,) = exchange(8, 0, last_rows, partial, [middle], [like(entering, BF16)], 4)
    (grad_out,) = exchange(0, 8, bare_rows, None, [cotangent], [], 5)
    through = cotangent
    terms, gain_terms = [None, None], [None, None]
    for layer in (1, 0):
        rows_attn, rotated, attended, log_total, rows_mlp, gate_up, hidden = saved[layer]
        partial, term_d, term_gu = mlp_backward(grad_out, rows_mlp, gate_up, hidden, weights[layer])
        grad_branch, grad_middle, mlp_term = exchange(
            8,
            4,
            back_rows,
            partial,
            [through, middles[layer], mlp_gains[layer]],
            [like(entering, F32), gain_like],
            9 - 3 * layer,
        )
        partial, term_attn = attn_backward(
            grad_branch, rows_attn, rotated, attended, log_total, weights[layer], owners, tables
        )
        back = [grad_middle, entered[layer], attn_gains[layer]]
        if layer == 1:
            grad_out, through, attn_term = exchange(
                4, 8, back_rows, partial, back, [like(entering, BF16), gain_like], 7
            )
        else:
            through, attn_term = exchange(
                4, 0, back_rows, partial, back, [like(entering, BF16), gain_like], 8
            )
        terms[layer] = (term_attn, term_gu, term_d)
        gain_terms[layer] = jnp.concatenate([attn_term, mlp_term], 0)

    sum_attn, sum_gu, sum_d = scattered_terms(terms, rows)
    query_half = w_query.shape[2] // 2
    kv_half = keyval_weight.shape[3]
    grad_attn = sum_attn.astype(F32).swapaxes(0, 1)
    grad_q = grad_attn[:, :, :query_half].reshape(w_query.shape)
    grad_kv = grad_attn[:, :, query_half : query_half + kv_half].reshape(rows, 2, 2, -1).swapaxes(1, 2)
    grad_o = grad_attn[:, :, query_half + kv_half :].reshape(w_out.shape)
    grad_gu = sum_gu.astype(F32).reshape(2, 2, rows, 2, -1).transpose(2, 3, 0, 1, 4)
    grad_d = sum_d.astype(F32).transpose(2, 0, 1, 3)

    gain_sum = reordered(jnp.stack(gain_terms))
    for place in [TENSOR, SECTION] + dp_bits():
        gain_sum = gain_sum + swap(gain_sum, place)
    own_gains = pick(gain_sum, section, 0)

    def half_columns(block):
        parts = reordered(block).reshape(seqs, here, 2, columns)
        kept = pick(parts, section, 2)
        other = swap(pick(parts, 1 - section, 2), SECTION)
        return pair(kept, other, SECTION, 0)

    layer_out = half_columns(last)
    in_grad = half_columns(through)
    return (
        layer_out,
        in_grad,
        own_gains[0][None],
        grad_q,
        grad_kv.reshape(keyval_weight.shape),
        grad_o,
        own_gains[1][None],
        grad_gu.reshape(w_gate_up.shape),
        grad_d.reshape(w_down.shape),
    )


def solution(mesh):
    activation = P(None, "dp", "tensor", "section")
    matrix = P("section", "dp", "tensor")
    stacked = P("section", "dp", None, "tensor")
    gain = P("section", None)
    return jax.shard_map(
        shards,
        mesh=mesh,
        in_specs=(
            activation,
            activation,
            P(None, "dp", None),
            gain,
            matrix,
            stacked,
            matrix,
            gain,
            stacked,
            matrix,
        ),
        out_specs=(
            activation,
            activation,
            gain,
            matrix,
            stacked,
            matrix,
            gain,
            stacked,
            matrix,
        ),
        check_vma=False,
    )
```

```python
import functools

import jax
import jax.numpy as jnp
from jax import lax
from jax.experimental import pallas as pl
from jax.experimental.pallas import tpu as pltpu
from jax.sharding import PartitionSpec as P

HEAD_SIZE = 64
NORM_EPSILON = 1e-05
ROPE_BASE = 10000.0
MASK_FILL = -1e30
FACTOR = HEAD_SIZE ** (-0.5)
BF16 = jnp.bfloat16
F32 = jnp.float32

def rope_tables(token_length):
    middle = HEAD_SIZE // 2
    frequency = ROPE_BASE ** (-(jnp.arange(middle, dtype=F32) * 2.0) / HEAD_SIZE)
    angles = frequency[:, None] * jnp.arange(token_length, dtype=F32)[None, :]
    return (
        jnp.concatenate([jnp.cos(angles), jnp.cos(angles)], 0),
        jnp.concatenate([jnp.sin(angles), jnp.sin(angles)], 0),
    )


def owners_of(lengths, token_length):
    bounds = jnp.cumsum(lengths, -1)
    places = jnp.arange(token_length, dtype=jnp.int32)
    return jnp.sum((places[None, :, None] >= bounds[:, None, :]).astype(jnp.int32), -1)


def visible_block(owner_col, owner_row):
    length = owner_col.shape[0]
    key_place = lax.broadcasted_iota(jnp.int32, (length, length), 0)
    query_place = lax.broadcasted_iota(jnp.int32, (length, length), 1)
    return (owner_col == owner_row) & (key_place <= query_place)


def rope(u, cosine, sine):
    half = HEAD_SIZE // 2
    return u * cosine + jnp.concatenate([-u[half:], u[:half]], 0) * sine


def rope_back(u, cosine, sine):
    half = HEAD_SIZE // 2
    w = u * sine
    return u * cosine + jnp.concatenate([w[half:], -w[:half]], 0)


def normed(values, gain):
    inverse = lax.rsqrt(jnp.mean(values * values, -1, keepdims=True) + NORM_EPSILON)
    return (values * inverse * gain).astype(BF16)


def norm_back(grad, values, gain):
    inverse = lax.rsqrt(jnp.mean(values * values, -1, keepdims=True) + NORM_EPSILON)
    scaled = values * inverse
    gained = grad * gain
    into = inverse * (gained - scaled * jnp.mean(gained * scaled, -1, keepdims=True))
    return into, jnp.sum(grad * scaled, 0, keepdims=True)


def crossed(values, group):
    count = values.shape[-1] // group
    return jnp.concatenate(
        [values[:, (g ^ 1) * group : ((g ^ 1) + 1) * group] for g in range(count)], 1
    )


def reordered(values, count):
    me = lax.axis_index("dp")
    group = values.shape[-1] // count
    while group < values.shape[-1]:
        values = jnp.where(lax.rem(me, 2) == 1, crossed(values, group), values)
        me, group = me // 2, group * 2
    return values


def dot_t(left, right):
    return lax.dot_general(left, right, (((1,), (1,)), ((), ())), preferred_element_type=F32)


def dot_n(left, right):
    return jnp.dot(left, right, preferred_element_type=F32)


def dot_tn(left, right):
    return lax.dot_general(left, right, (((0,), (0,)), ((), ())), preferred_element_type=F32)


class Hops:
    def __init__(self, send, recv):
        self.send, self.recv, self.count, self.started = send, recv, 0, []
        self.index = {name: lax.axis_index(name) for name in ("section", "dp", "tensor")}
        self.other = 1 - self.index["section"]

    def to(self, offset):
        dp = self.index["dp"]
        for bit in range(offset.bit_length()):
            if offset >> bit & 1:
                low = lax.rem(dp // (1 << bit), 2)
                dp = dp + (1 - 2 * low) * (1 << bit)
        return (self.index["section"], dp, self.index["tensor"])

    def across(self):
        return (self.other, self.index["dp"], self.index["tensor"])

    def core(self):
        return (self.index["section"], self.index["dp"], 1 - self.index["tensor"])

    def at(self, source, target, device, index):
        return pltpu.make_async_remote_copy(
            src_ref=source,
            dst_ref=target,
            send_sem=self.send.at[index],
            recv_sem=self.recv.at[index],
            device_id=device,
            device_id_type=pl.DeviceIdType.MESH,
        )

    def claim(self, number=1):
        self.count += number
        return self.count - number

    def start(self, source, target, device):
        copy = self.at(source, target, device, self.claim())
        copy.start()
        self.started.append(copy)
        return copy

    def start_either(self, choice, first, second, target, device):
        index = self.claim()
        copy = self.at(first, target, device, index)
        backup = self.at(second, target, device, index)
        pl.when(choice)(copy.start)
        pl.when(jnp.logical_not(choice))(backup.start)
        self.started.append(copy)
        return copy

    def sent(self, copies):
        copies = list(copies)
        for copy in copies:
            copy.wait_send()
        gone = {id(copy) for copy in copies}
        self.started = [copy for copy in self.started if id(copy) not in gone]

    def greet(self, offsets):
        barrier = pltpu.get_barrier_semaphore()
        devices = [self.to(offset) for offset in offsets] + [self.across(), self.core()]
        for device in devices:
            pl.semaphore_signal(
                barrier, inc=1, device_id=device, device_id_type=pl.DeviceIdType.MESH
            )
        pl.semaphore_wait(barrier, len(devices))

    def drain(self):
        for copy in self.started:
            copy.wait_send()


class Local:
    AT_ONCE = 6

    def __init__(self, sems):
        self.sems, self.count = sems, self.AT_ONCE

    def claim(self, number=1):
        self.count += number
        return self.count - number

    def make(self, source, target):
        return pltpu.make_async_copy(source, target, self.sems.at[self.claim()])

    def start(self, source, target):
        copy = self.make(source, target)
        copy.start()
        return copy

    def now(self, *moves):
        waits = []
        for index, move in enumerate(moves):
            make = lambda source: pltpu.make_async_copy(source, move[-1], self.sems.at[index])
            copy = make(move[-2])
            if len(move) == 2:
                copy.start()
            else:
                pl.when(move[0])(make(move[1]).start)
                pl.when(jnp.logical_not(move[0]))(copy.start)
            waits.append(copy)
        for copy in waits:
            copy.wait()


def reached(count):
    return [1] + [2 * k for k in range(1, count // 2)]


class Spread:
    def __init__(self, hops, local, own, turned, group):
        self.hops, self.local, self.own, self.turned, self.group = hops, local, own, turned, group

    def four(self, rows, slots):
        hops, own = self.hops, self.own
        section, tensor = hops.index["section"], hops.index["tensor"]
        own[...] = rows
        slot = 2 * section + tensor
        self.over_y = hops.start(own, slots.at[slot], hops.across())
        self.over_core = hops.start(own, slots.at[slot], hops.core())
        self.keep = self.local.start(own, slots.at[slot])

    def four_end(self, slots):
        hops = self.hops
        self.over_y.wait_recv()
        across = 2 * (1 - hops.index["section"]) + hops.index["tensor"]
        last = hops.start(slots.at[across], slots.at[across], hops.core())
        self.over_core.wait_recv()
        last.wait_recv()
        self.keep.wait()
        hops.sent([self.over_y, self.over_core, last])

    def halves(self):
        half = self.own.shape[0] // 2
        return pl.ds(0, half), pl.ds(half, half)

    def eight(self, rows, slots):
        hops, own, turned = self.hops, self.own, self.turned
        own[...] = rows
        turned[...] = crossed(rows, self.group)
        lo, hi = self.halves()
        y, z, core = hops.across(), hops.to(2), hops.core()
        self.over = [
            hops.start(own.at[hi], slots.at[2, hi], y),
            hops.start(turned.at[lo], slots.at[4, lo], z),
            hops.start(own.at[lo], slots.at[2, lo], y),
            hops.start(turned.at[hi], slots.at[4, hi], z),
        ]
        self.cores = [hops.start(own, slots.at[1], core)]
        self.keep = self.local.start(own, slots.at[0])

    def eight_middle(self, slots):
        hops, group = self.hops, self.group
        lo, hi = self.halves()
        self.over[0].wait_recv()
        self.diag = [
            hops.start(
                slots.at[2, hi, pl.ds(g * group, group)],
                slots.at[6, hi, pl.ds((g ^ 1) * group, group)],
                hops.to(2),
            )
            for g in range(self.own.shape[1] // group)
        ]
        self.over[1].wait_recv()
        self.diag.append(hops.start(slots.at[4, lo], slots.at[6, lo], hops.across()))

    def eight_end(self, slots):
        hops = self.hops
        core = hops.core()
        self.over[2].wait_recv()
        self.cores.append(hops.start(slots.at[2], slots.at[3], core))
        self.over[3].wait_recv()
        self.cores.append(hops.start(slots.at[4], slots.at[5], core))
        for copy in self.diag:
            copy.wait_recv()
        self.cores.append(hops.start(slots.at[6], slots.at[7], core))
        for copy in self.cores:
            copy.wait_recv()
        self.keep.wait()
        hops.sent(self.over + self.diag + self.cores)


class Sums:
    def __init__(self, hops, partial, core, out, from_y, from_z, part_y, part_z, group):
        self.hops, self.partial, self.core, self.out, self.group = hops, partial, core, out, group
        self.from_y, self.from_z, self.part_y, self.part_z = from_y, from_z, part_y, part_z

    def four(self):
        hops, core, out, from_y, partial = self.hops, self.core, self.out, self.from_y, self.partial
        section, tensor = hops.index["section"], hops.index["tensor"]
        slots = [2 * section, 2 * (1 - section)]
        far = {
            c: hops.start(partial.at[slots[c] + 1 - tensor], core.at[c], hops.core()) for c in (1, 0)
        }
        far[1].wait_recv()
        out[0] = (partial[slots[1] + tensor].astype(F32) + core[1].astype(F32)).astype(BF16)
        over_y = hops.start(out.at[0], from_y, hops.across())
        far[0].wait_recv()
        over_y.wait_recv()
        total = (
            partial[slots[0] + tensor].astype(F32) + core[0].astype(F32) + from_y[...].astype(F32)
        )
        hops.sent([far[0], far[1], over_y])
        return total

    def halves(self):
        half = self.out.shape[1] // 2
        return pl.ds(0, half), pl.ds(half, half)

    def added(self, c, rows):
        return self.partial[2 * c, rows, :].astype(F32) + self.core[c, rows, :].astype(F32)

    def eight(self):
        hops, out, group = self.hops, self.out, self.group
        lo, hi = self.halves()
        y, z = hops.across(), hops.to(2)
        self.far = {
            c: hops.start(self.partial.at[2 * c + 1], self.core.at[c], hops.core())
            for c in (3, 1, 2, 0)
        }
        self.far[3].wait_recv()
        out[2, lo, :] = self.added(3, lo).astype(BF16)
        self.diag_y = hops.start(out.at[2, lo], self.part_y, y)
        out[2, hi, :] = crossed(self.added(3, hi), group).astype(BF16)
        self.diag_z = hops.start(out.at[2, hi], self.part_z, z)
        self.far[1].wait_recv()
        out[0, lo, :] = self.added(1, lo).astype(BF16)
        self.over = [hops.start(out.at[0, lo], self.from_y.at[lo], y)]
        self.far[2].wait_recv()
        out[1, hi, :] = crossed(self.added(2, hi), group).astype(BF16)
        self.over.append(hops.start(out.at[1, hi], self.from_z.at[hi], z))

    def eight_middle(self):
        hops, out, group = self.hops, self.out, self.group
        lo, hi = self.halves()
        self.diag_y.wait_recv()
        out[1, lo, :] = crossed(self.added(2, lo) + self.part_y[...].astype(F32), group).astype(BF16)
        self.over.append(hops.start(out.at[1, lo], self.from_z.at[lo], hops.to(2)))
        self.diag_z.wait_recv()
        out[0, hi, :] = (self.added(1, hi) + self.part_z[...].astype(F32)).astype(BF16)
        self.over.append(hops.start(out.at[0, hi], self.from_y.at[hi], hops.across()))

    def eight_end(self):
        self.far[0].wait_recv()
        for copy in self.over:
            copy.wait_recv()
        total = (
            self.partial[0].astype(F32)
            + self.core[0].astype(F32)
            + self.from_y[...].astype(F32)
            + self.from_z[...].astype(F32)
        )
        self.hops.sent(list(self.far.values()) + [self.diag_y, self.diag_z] + self.over)
        return total


QKV, OUT, GU, DOWN = range(4)
IS_SHARED = (False, False, True, True)


def others(k, kinds):
    return [k] + (list(range(4, kinds)) if k == 1 else [])


class Gather:
    def __init__(self, hops, local, count, packs, crossed_over, full):
        self.hops, self.local, self.packs, self.over, self.full = hops, local, packs, crossed_over, full
        self.kinds = count // 2
        self.arrived, self.have = {}, set()
        self.half = lax.rem(hops.index["dp"] // 2, 2)
        self.rows = packs[0].shape[-2]

    def cross(self, a):
        hops = self.hops
        self.arrived[a] = hops.start(self.packs[a].at[hops.other], self.over[a], hops.across())

    def block(self, a, layer, r):
        return self.full[layer][a].at[pl.ds(r * self.rows, self.rows)]

    def source(self, a, other):
        if a not in self.have:
            self.have.add(a)
            self.arrived[a].wait_recv()
        section = self.hops.index["section"]
        if not IS_SHARED[a]:
            return self.packs[a].at[section], self.over[a]
        which = 1 - self.half if other else self.half
        return self.packs[a].at[section, which], self.over[a].at[which]

    def straight(self, a, layer):
        first, second = self.source(a, False)
        here = self.hops.index["section"] == layer
        self.arrived[a, layer, "x", 0] = self.hops.start_either(
            here, first, second, self.block(a, layer, 1), self.hops.to(1)
        )

    def begin(self, a, layer, step):
        for k in others(step, self.kinds):
            if IS_SHARED[a] or k == 1 or k % 2 == 0:
                first, second = self.source(a, k % 2 == 1)
                self.arrived[a, layer, k] = self.hops.start_either(
                    self.hops.index["section"] == layer,
                    first,
                    second,
                    self.block(a, layer, 2 * k),
                    self.hops.to(2 * k),
                )

    def onward(self, a, layer, step):
        hops = self.hops
        for k in others(step, self.kinds):
            self.arrived[a, layer, k].wait_recv()
            self.arrived[a, layer, "x", k] = hops.start(
                self.block(a, layer, 2 * k), self.block(a, layer, 2 * k + 1), hops.to(1)
            )
            if not IS_SHARED[a] and k % 2 == 0:
                self.arrived[a, layer, k + 1] = hops.start(
                    self.block(a, layer, 2 * k), self.block(a, layer, 2 * k + 2), hops.to(2)
                )

    def complete(self, a, layer):
        for k in range(self.kinds):
            self.arrived[a, layer, "x", k].wait_recv()

    def parts(self, a, layer, target):
        first, second = self.source(a, False)
        rest = pl.ds(self.rows, target.shape[0] - self.rows)
        here = self.hops.index["section"] == layer
        return [
            (here, first, second, target.at[pl.ds(0, self.rows)]),
            (self.full[layer][a].at[rest], target.at[rest]),
        ]


def attention_step(heads, qkv, place, cos, sin, visible, rotated, log_total):
    width = heads * HEAD_SIZE
    keys = rope(qkv[width : width + HEAD_SIZE, place], cos, sin).astype(BF16)
    values = qkv[width + HEAD_SIZE :, place].astype(BF16)
    rotated[width : width + HEAD_SIZE, place] = keys
    rotated[width + HEAD_SIZE :, place] = values
    attended = []
    for h in range(heads):
        at = slice(h * HEAD_SIZE, (h + 1) * HEAD_SIZE)
        queries = rope(qkv[at, place], cos, sin).astype(BF16)
        rotated[at, place] = queries
        score = dot_tn(keys, queries)
        score = jnp.where(visible, score * FACTOR, MASK_FILL)
        top = jnp.max(score, 0, keepdims=True)
        exponent = jnp.exp(score - top)
        total = jnp.sum(exponent, 0, keepdims=True)
        prob = (exponent * (1.0 / total)).astype(BF16)
        attended.append(dot_n(values, prob))
        log_total[h : h + 1, place] = top + jnp.log(total)
    return jnp.concatenate(attended, 0).T.astype(BF16)


def attention_back_step(heads, rotated, grad_att, place, cos, sin, visible, log_total):
    width = heads * HEAD_SIZE
    keys = rotated[width : width + HEAD_SIZE, place]
    values = rotated[width + HEAD_SIZE :, place]
    length = keys.shape[1]
    grad_keys = jnp.zeros((HEAD_SIZE, length), F32)
    grad_values = jnp.zeros((HEAD_SIZE, length), F32)
    found = []
    for h in range(heads):
        at = slice(h * HEAD_SIZE, (h + 1) * HEAD_SIZE)
        queries = rotated[at, place]
        grad = grad_att[at, :]
        score = jnp.where(visible, dot_tn(keys, queries) * FACTOR, MASK_FILL)
        prob = jnp.exp(score - log_total[h : h + 1, place])
        grad_prob = dot_tn(values, grad)
        inner = jnp.sum(prob * grad_prob, 0, keepdims=True)
        grad_score = (FACTOR * prob * (grad_prob - inner)).astype(BF16)
        found.append(rope_back(dot_n(keys, grad_score), cos, sin))
        grad_keys += dot_t(queries, grad_score)
        grad_values += dot_t(grad, prob.astype(BF16))
    found += [rope_back(grad_keys, cos, sin), grad_values]
    return jnp.concatenate(found, 0).T.astype(BF16)


def steps_of(names):
    found = []
    for name in names:
        letters = name.rstrip("0123456789")
        found.append((letters, *(int(digit) for digit in name[len(letters) :])))
    return found


ORDER = (
    "c0", "c1", "B002", "B001", "B012", "c2", "O001", "O002", "B102", "c3", "B112", "X20",
    "O003", "B101", "O102", "B302", "n0", "m0", "X00", "a0", "B201", "X30", "B301", "X01",
    "X10", "O112", "B203", "O103", "B303", "O101", "B202", "e0", "O201", "q0", "O302", "O203",
    "X11", "r0", "g0", "O303", "h0", "B111", "O202", "B011", "O301", "X21", "B213", "i0",
    "B312", "O011", "u0", "d0", "s0", "O111", "t0", "O012", "O113", "B211", "B311", "v0",
    "a1", "n1", "O013", "B212", "X31", "e1", "O213", "q1", "O211", "r1", "g1", "h1",
    "B313", "O212", "O311", "O312", "m1", "i1", "g2", "u1", "h2", "O313", "i2", "bl1",
    "S31", "E31", "bk1", "bp1", "bs1", "S21", "bt1", "Z313", "Z310", "Z311", "Z312", "bv1",
    "E21", "ba1", "Z211", "be1", "bq1", "Z212", "E11", "S01", "E01", "br1", "bg1", "bh1",
    "Z011", "Z213", "Y31", "S11", "Z013", "bi1", "bl0", "S30", "bk0", "Z210", "Z110", "Z113",
    "Y21", "E30", "Z111", "Z012", "bp0", "bs0", "Z302", "S20", "bt0", "E20", "Z300", "Z301",
    "Z112", "bv0", "ba0", "Z010", "Z303", "Z201", "Y11", "Y01", "be0", "Z202", "bq0", "S00",
    "S10", "br0", "bn0", "bn1", "Y30", "E10", "Z203", "E00", "Z003", "d1", "Z001", "Z200",
    "bn2", "s1", "Z002", "Z103", "Y20", "Z000", "Z101", "bn3", "Z100", "Z102", "Y00", "bn4",
    "t1", "Y10", "v1", "bn5", "w0", "w1",
)


def into_partial(block, w, partial, here, width, tile):
    @pl.loop(0, width // tile)
    def _(n):
        cut = pl.ds(pl.multiple_of(n * tile, tile), tile)
        some = dot_t(block[...], w[cut, :])
        partial[:, :, cut] = some.astype(BF16).reshape(partial.shape[0], here, tile)


def add_rows(target, left, right):
    rows = target.shape[0]
    step = min(32, rows)

    @pl.loop(0, rows // step)
    def _(i):
        at = pl.ds(pl.multiple_of(i * step, step), step)
        target[at, :] = (left[at, :].astype(F32) + right[at, :].astype(F32)).astype(BF16)


class Scatter:
    def __init__(self, hops, local, kept, staged, landed, distant, sums_out, one_block, term, rows):
        self.hops, self.local, self.kept, self.staged = hops, local, kept, staged
        self.landed, self.distant, self.sums_out = landed, distant, sums_out
        self.one_block, self.term, self.rows = one_block, term, rows
        self.kinds = kept[0].shape[0]
        self.half = lax.rem(hops.index["dp"] // 2, 2)
        self.section = hops.index["section"]
        self.copies, self.ending = {}, []

    def renew(self, a):
        assert (a, 1) in [entry[:2] for entry in self.ending]
        out = [self.copies[a, 1, "z", k] for k in range(1, self.kinds)]
        self.hops.sent([copy for copy in out if copy is not None])
        for b, layer, keep, away in self.ending:
            if (b, layer) == (a, 1):
                pl.when(self.section == layer)(keep.wait)
                pl.when(self.section != layer)(away.wait_send)

    def stage(self, a, layer):
        hops, local, rows, kept = self.hops, self.local, self.rows, self.kept
        if layer == 0 and rows % 128:
            self.renew(a)
        base, at = hops.claim(self.kinds), local.claim(self.kinds)
        cols = pl.ds(0, kept[a].shape[-1])
        source, target = self.staged[layer][a], self.landed[layer][a]

        @pl.loop(0, self.kinds)
        def _(k):
            if rows % 128:
                both = self.term(a, 2 * k, 2 * rows)
                self.one_block[:, cols] = both[rows:]
                kept[a][k] = both[:rows]
            else:
                self.one_block[:, cols] = self.term(a, 2 * k + 1, rows)
            keep = pltpu.make_async_copy(
                self.one_block.at[:, cols], source.at[k], local.sems.at[at + k]
            )
            keep.start()
            keep.wait()
            hops.at(source.at[k], target.at[k], hops.to(1), base + k).start()

        for k in range(self.kinds):
            copy = hops.at(source.at[k], target.at[k], hops.to(1), base + k)
            self.copies[a, layer, "x", k] = copy
            hops.started.append(copy)

    def evens(self, a, layer):
        if self.rows % 128:
            return
        if layer == 0:
            self.renew(a)

        @pl.loop(0, self.kinds)
        def _(k):
            self.kept[a][k] = self.term(a, 2 * k, self.rows)

    def fetch(self, a, source):
        block = self.one_block.at[:, pl.ds(0, self.kept[a].shape[-1])]
        self.local.now((source, block))
        return block

    def meet(self, a, layer, step):
        hops, kept, copies = self.hops, self.kept[a], self.copies
        far = self.distant[layer][a]
        steps = [0] if step == 0 else list(reversed(others(step, self.kinds)))
        for k in steps:
            copies[a, layer, "x", k].wait_recv()
            add_rows(kept.at[k], kept.at[k], self.fetch(a, self.landed[layer][a].at[k]))
            if not IS_SHARED[a] and k % 2 == 0 and k:
                copies[a, layer, "z", k + 1].wait_recv()
                add_rows(kept.at[k], kept.at[k], self.fetch(a, far.at[k + 1]))
            if k:
                passed = not IS_SHARED[a] and k % 2 == 1 and k > 1
                copies[a, layer, "z", k] = hops.start(
                    kept.at[k], far.at[k], hops.to(2 if passed else 2 * k)
                )

    def deliver(self, a, layer):
        hops, kept, copies = self.hops, self.kept[a], self.copies
        far = self.distant[layer][a]
        mine, other = [], []
        for k in range(1, self.kinds):
            if IS_SHARED[a] or k == 1 or k % 2 == 0:
                copies[a, layer, "z", k].wait_recv()
                (other if IS_SHARED[a] and k % 2 else mine).append(k)
        for k in mine:
            add_rows(kept.at[0], kept.at[0], self.fetch(a, far.at[k]))
        pieces = [kept.at[0]]
        if IS_SHARED[a]:
            hops.sent([copies[a, layer, "z", 1]])
            copies[a, layer, "z", 1] = None
            self.local.now((far.at[other[0]], kept.at[1]))
            for k in other[1:]:
                add_rows(kept.at[1], kept.at[1], self.fetch(a, far.at[k]))
            pieces.append(kept.at[1])
        for number, piece in enumerate(pieces):
            which = self.half if number == 0 else 1 - self.half
            target = self.sums_out[a].at[self.section]
            if IS_SHARED[a]:
                target = self.sums_out[a].at[self.section, which]
            keep = self.local.make(piece, target)
            away = hops.at(piece, target, hops.across(), hops.claim())
            pl.when(self.section == layer)(keep.start)
            pl.when(self.section != layer)(away.start)
            self.ending.append((a, layer, keep, away))

    def end(self):
        for a, layer, keep, away in self.ending:
            pl.when(self.section == layer)(away.wait_recv)
            if layer == 0:
                pl.when(self.section == layer)(keep.wait)
                pl.when(self.section != layer)(away.wait_send)


def layers_kernel(count, heads, group, *refs):
    refs = list(refs)
    take = lambda number: [refs.pop(0) for _ in range(number)]
    packs, raw_rows, raw_gains = take(4), take(2), take(2)
    cosine, sine, owner_col, owner_row = take(4)
    ends, sums_out = take(2), take(4)
    crossed_over, full = take(4), (take(4), take(4))
    rows_attn_out, hidden_out, (rows_mlp_out, gate_up_out, grad_out) = take(2), take(2), take(3)
    staged, landed, distant = [(take(4), take(4)) for _ in range(3)]
    gain_sums = take(2)
    send, recv, sems = take(3)
    w_low, w_out, w_gu = take(3)
    slots4, slots8, partial, rows_mlp = take(4)
    qkv, gate_up, hidden = take(3)
    rotated, attended, log_total, middles = [take(2) for _ in range(4)]
    grad_att, grad_qkv = take(2)
    kept, (one_block,) = take(4), take(1)
    entering, handed, grad_middle = take(3)
    raw_whole, cotangent, through = take(3)
    gain_whole, gains, gain_terms, gain_landed = take(4)
    own, turned, core, out, from_y, from_z, part_y, part_z, last_z, last_part = take(10)
    hops, local = Hops(send, recv), Local(sems)
    hops.greet(reached(count))
    spread = Spread(hops, local, own, turned, group)
    sums = Sums(hops, partial, core, out, from_y, from_z, part_y, part_z, group)
    sums_last = Sums(hops, partial, core, out, from_y, last_z, part_y, last_part, group)
    gather = Gather(hops, local, count, packs, crossed_over, full)
    section = hops.index["section"]
    here, width = own.shape
    rows = width // count
    length = cosine.shape[1]
    seqs = slots4.shape[0] * here // length
    per_seq = length // here
    tile = 512
    units = hidden.shape[1]
    real = gate_up.shape[1] // 2
    whole = real // 128
    rest = real - whole * 128
    split = rotated[0].shape[0]
    rows_attn = partial.at[pl.ds(4, 4)]
    stores = []

    def store(source, target):
        stores.append(local.start(source, target))

    def settle():
        for copy in stores:
            copy.wait()
        stores.clear()

    def span(i, size):
        return pl.ds(pl.multiple_of(i * size, size), size)

    w_qkv = w_low.at[:, pl.ds(0, split)]

    def project(layer):
        gather.complete(QKV, layer)
        gather.complete(OUT, layer)
        local.now(*gather.parts(QKV, layer, w_qkv), *gather.parts(OUT, layer, w_out))

        @pl.loop(0, seqs)
        def _(i):
            block = slots4[pl.ds(i * per_seq, per_seq)].reshape(length, width)
            place = span(i, length)
            qkv[:, place] = dot_n(block, w_low[:, :split]).T
            visible = visible_block(owner_col[i], owner_row[i])
            attended[layer][place, :] = attention_step(
                heads, qkv, place, cosine[...], sine[...], visible, rotated[layer], log_total[layer]
            )

        store(slots4, rows_attn_out[layer])

        @pl.loop(0, width // tile)
        def _(n):
            cut = span(n, tile)
            for i in range(seqs):
                some = dot_t(attended[layer][i * length : (i + 1) * length, :], w_out[cut, :])
                partial[i * per_seq : (i + 1) * per_seq, :, cut] = some.astype(BF16).reshape(
                    per_seq, here, tile
                )

    def expand(layer):
        gather.complete(GU, layer)
        local.now(*gather.parts(GU, layer, w_gu))

        block = slots8[...].reshape(slots8.shape[0] * here, width)

        @pl.loop(0, whole)
        def _(n):
            cut = span(n, 256)
            both = dot_n(block, w_gu[:, cut])
            gate_up[:, cut] = both.astype(BF16)
            gate, up = both[:, :128], both[:, 128:]
            hidden[:, span(n, 128)] = (gate * jax.nn.sigmoid(gate) * up).astype(BF16)

        if rest:
            both = dot_n(block, w_gu[:, whole * 256 :])
            gate_up[:, whole * 256 :] = both.astype(BF16)
            gate, up = both[:, :rest], both[:, rest:]
            some = (gate * jax.nn.sigmoid(gate) * up).astype(BF16)
            hidden[:, whole * 128 :] = jnp.concatenate([some, jnp.zeros_like(some)], 1)

        if layer == 0:
            store(slots8, rows_mlp_out)
            store(gate_up, gate_up_out)
        else:
            rows_mlp[...] = slots8[...]
        store(hidden, hidden_out[layer])

    def entry(layer):
        return entering if layer == 0 else handed

    waiting = {}

    def bring(number):
        target = raw_whole.at[:, span(section, width // 2)]
        waiting[number] = [
            hops.start(raw_rows[number].at[hops.other, 0], target, hops.across()),
            local.start(raw_rows[number].at[section, 0], target),
        ]
        if number == 0:
            for kind in range(2):
                waiting[number] += [
                    hops.start(raw_gains[kind], gain_whole.at[section, kind], hops.across()),
                    local.start(raw_gains[kind], gain_whole.at[section, kind]),
                ]

    def brought(number):
        for place, copy in enumerate(waiting[number]):
            copy.wait() if place % 2 else copy.wait_recv()
        rows_here = reordered(raw_whole[...].astype(F32), count)
        if number == 0:
            entering[...] = rows_here
            for layer in range(2):
                for kind in range(2):
                    mark = 2 * layer + kind
                    gains[mark : mark + 1, :] = reordered(gain_whole[layer, kind], count)
        else:
            cotangent[...] = rows_here.astype(BF16)

    def gain(layer, kind):
        mark = 2 * layer + kind
        return gains[mark : mark + 1, :]

    def ready(layer):
        settle()
        if layer == 1:
            local.now((grad_out, slots8))
        else:
            local.now((gate_up_out, gate_up), (hidden_out[0], hidden), (rows_mlp_out, rows_mlp))

    def widen(layer):
        if layer == 1:
            gather.complete(DOWN, 1)
        local.now(*gather.parts(DOWN, layer, w_low))

        @pl.loop(0, slots8.shape[0] // 2)
        def _(c):
            block = slots8[pl.ds(c * 2, 2)].reshape(2 * here, width)
            place = span(c, 2 * here)
            grad_hidden = dot_n(block, w_low[...]).astype(BF16).astype(F32)

            def back(grad, gate, up):
                gate, up = gate.astype(F32), up.astype(F32)
                sig = jax.nn.sigmoid(gate)
                return [
                    (grad * up * sig * (1.0 + gate * (1.0 - sig))).astype(BF16),
                    (grad * (gate * sig)).astype(BF16),
                ]

            for n in range(whole):
                at = slice(n * 256, n * 256 + 256)
                both = gate_up[place, at]
                gate_up[place, at] = jnp.concatenate(
                    back(grad_hidden[:, n * 128 : n * 128 + 128], both[:, :128], both[:, 128:]), 1
                )
            if rest:
                both = gate_up[place, whole * 256 :]
                gate_up[place, whole * 256 :] = jnp.concatenate(
                    back(grad_hidden[:, whole * 128 : real], both[:, :rest], both[:, rest:]), 1
                )

    def attend(layer):
        local.now(
            *gather.parts(OUT, layer, w_out),
            *gather.parts(QKV, layer, w_qkv),
            (rows_attn_out[layer], rows_attn),
        )

        @pl.loop(0, seqs)
        def _(i):
            block = slots4[pl.ds(i * per_seq, per_seq)].reshape(length, width)
            place = span(i, length)
            grad_att[...] = dot_n(block, w_out[...]).T.astype(BF16)
            visible = visible_block(owner_col[i], owner_row[i])
            grad_qkv[place, :] = attention_back_step(
                heads, rotated[layer], grad_att, place, cosine[...], sine[...], visible, log_total[layer]
            )

        @pl.loop(0, width // tile)
        def _(n):
            cut = span(n, tile)
            for i in range(seqs):
                some = dot_t(grad_qkv[i * length : (i + 1) * length, :], w_low[cut, :split])
                partial[i * per_seq : (i + 1) * per_seq, :, cut] = some.astype(BF16).reshape(
                    per_seq, here, tile
                )

    working = [1]

    def term(a, r, size):
        slots, right = {
            QKV: (rows_attn, grad_qkv),
            OUT: (slots4, attended[working[0]]),
            GU: (rows_mlp, gate_up),
            DOWN: (slots8, hidden),
        }[a]
        cut = pl.ds(pl.multiple_of(r * rows, max(rows, 128)), size)
        return dot_tn(slots[:, :, cut].reshape(slots.shape[0] * here, size), right[...]).astype(BF16)

    scatter = Scatter(
        hops, local, kept, staged, landed, distant, sums_out, one_block, term, rows
    )

    def back_through(total, source, values, layer, kind, result):
        into, term_row = norm_back(total, values, gain(layer, kind))
        mark = 2 * layer + kind
        gain_terms[0, mark : mark + 1, :] = term_row
        result[...] = (source + into).astype(result.dtype)

    leaving = []

    def leave(number, block):
        block[...] = reordered(block[...].astype(F32), count).astype(BF16)
        target = ends[number].at[section, 0]
        leaving.append(local.start(block.at[:, span(section, width // 2)], target))
        leaving.append(hops.start(block.at[:, span(hops.other, width // 2)], target, hops.across()))

    gain_places, offset = [hops.core(), hops.across()], 1
    while offset < count:
        gain_places.append(hops.to(offset))
        offset *= 2
    gain_moves = []

    def add_gains(step):
        for number in range(step, len(gain_places) + 1) if step == 5 else [step]:
            if number == 0:
                gain_terms[0] = reordered(gain_terms[0], count)
            else:
                gain_moves[-1].wait_recv()
                gain_terms[number] = gain_terms[number - 1] + gain_landed[number - 1]
            if number < len(gain_places):
                gain_moves.append(
                    hops.start(gain_terms.at[number], gain_landed.at[number], gain_places[number])
                )
        if step == 5:
            total = gain_terms[len(gain_places)]
            mine = jnp.where(section == 0, total[0:2], total[2:4])
            for kind in range(2):
                gain_sums[kind][...] = mine[kind : kind + 1]

    for name, *at in steps_of(ORDER):
        layer = at[0]
        if name == "c":
            gather.cross(*at)
        elif name == "X":
            gather.straight(*at)
        elif name == "B":
            gather.begin(*at)
        elif name == "O":
            gather.onward(*at)
        elif name == "n":
            bring(*at)
        elif name == "m":
            brought(*at)
        elif name == "a":
            spread.four(normed(entry(layer)[...], gain(layer, 0)), slots4)
        elif name in ("e", "be"):
            spread.four_end(slots4)
        elif name == "q":
            project(layer)
        elif name == "r":
            middles[layer][...] = entry(layer)[...] + sums.four()
        elif name == "g":
            if layer == 2:
                spread.eight(cotangent[...], grad_out)
            else:
                spread.eight(normed(middles[layer][...], gain(layer, 1)), slots8)
        elif name == "h":
            spread.eight_middle(grad_out if layer == 2 else slots8)
        elif name == "i":
            spread.eight_end(grad_out if layer == 2 else slots8)
        elif name == "u":
            expand(layer)
        elif name == "d":
            if layer == 0:
                gather.complete(DOWN, 0)
            else:
                local.now((hidden_out[1], hidden))
            local.now(*gather.parts(DOWN, layer, w_low))
            into_partial(hidden, w_low, partial, here, width, tile // 2)
        elif name == "s":
            settle()
            (sums_last if layer == 1 else sums).eight()
        elif name == "t":
            (sums_last if layer == 1 else sums).eight_middle()
        elif name == "v":
            if layer == 1:
                raw_whole[...] = (middles[1][...] + sums_last.eight_end()).astype(BF16)
            else:
                handed[...] = (middles[0][...] + sums.eight_end()).astype(BF16).astype(F32)
        elif name == "bl":
            working[0] = layer
            ready(layer)
        elif name == "bk":
            widen(layer)
        elif name == "S":
            scatter.stage(*at)
        elif name == "E":
            scatter.evens(*at)
        elif name == "Z":
            scatter.meet(*at)
        elif name == "Y":
            scatter.deliver(*at)
        elif name == "bp":
            if layer == 0:
                local.now(*gather.parts(GU, 0, w_gu))
            into_partial(gate_up, w_gu, partial, here, width, tile // 2)
        elif name == "bs":
            sums.eight()
        elif name == "bt":
            sums.eight_middle()
        elif name == "bv":
            total = sums.eight_end()
            source = (cotangent if layer == 1 else through)[...].astype(F32)
            back_through(total, source, middles[layer][...], layer, 1, grad_middle)
        elif name == "ba":
            spread.four(grad_middle[...].astype(BF16), slots4)
        elif name == "bq":
            attend(layer)
        elif name == "br":
            back_through(sums.four(), grad_middle[...], entry(layer)[...], layer, 0, through)
        elif name == "bg":
            spread.eight(through[...], slots8)
        elif name == "bh":
            spread.eight_middle(slots8)
        elif name == "bi":
            spread.eight_end(slots8)
        elif name == "w":
            leave(layer, (raw_whole, through)[layer])
        elif name == "bn":
            add_gains(layer)
    scatter.end()
    settle()
    for place, copy in enumerate(leaving):
        copy.wait_recv() if place % 2 else copy.wait()
    hops.drain()


def both_layers(packs, raw, tables, owners):
    count = lax.axis_size("dp")
    kinds = count // 2
    anywhere = pl.BlockSpec(memory_space=pl.ANY)
    inside = pl.BlockSpec(memory_space=pltpu.VMEM)
    seqs, length = owners.shape
    tokens = seqs * length
    here, width = tokens // 4, packs[0].shape[-2] * count
    rows = width // count
    columns = [pack.shape[-1] for pack in packs]
    head_width = columns[OUT]
    heads = head_width // HEAD_SIZE
    group = 2 * width // count
    shape = lambda *dims: jax.ShapeDtypeStruct(dims, BF16)
    ends = [shape(*raw[0].shape)] * 2
    sums = [shape(*((2, 2) if IS_SHARED[a] else (2,)), rows, columns[a]) for a in range(4)]
    full = [shape(width, columns[a]) for a in range(4)] * 2
    rest = (
        [shape(4, here, width)] * 2
        + [shape(8 * here, columns[DOWN])] * 2
        + [shape(8, here, width), shape(8 * here, columns[GU]), shape(8, here, width)]
    )
    blocks = [shape(kinds, rows, columns[a]) for a in range(4)] * 6
    far = ends + sums + [shape(*pack.shape[1:]) for pack in packs] + full + rest + blocks
    near = [jax.ShapeDtypeStruct((1, width), F32)] * 2
    inner = lambda *dims: pltpu.VMEM(dims, BF16)
    block = lambda *lead: pltpu.VMEM(lead + (here, width), BF16)
    wide = pltpu.VMEM((here, width), F32)
    wires = 2 * 8 * count + 8 * kinds + 6 * (12 + width // group) + 80
    scratch = [
        pltpu.SemaphoreType.DMA((wires,)),
        pltpu.SemaphoreType.DMA((wires,)),
        pltpu.SemaphoreType.DMA((8 * kinds + 60,)),
        inner(width, columns[DOWN]),
        inner(width, columns[OUT]),
        inner(width, columns[GU]),
        block(4),
        block(8),
        block(8),
        block(8),
        pltpu.VMEM((columns[QKV], tokens), F32),
        inner(8 * here, columns[GU]),
        inner(8 * here, columns[DOWN]),
    ]
    scratch += [inner(columns[QKV], tokens)] * 2 + [inner(tokens, head_width)] * 2
    scratch += [pltpu.VMEM((heads, tokens), F32)] * 2 + [wide] * 2
    scratch += [inner(head_width, length), inner(tokens, columns[QKV])]
    scratch += [inner(kinds, rows, columns[a]) for a in range(4)] + [inner(rows, max(columns))]
    scratch += [wide] * 3 + [block()] * 3
    sums_of = count.bit_length() + 1
    scratch += [
        pltpu.VMEM((2, 2, 1, width), F32),
        pltpu.VMEM((4, width), F32),
        pltpu.VMEM((sums_of + 1, 4, width), F32),
        pltpu.VMEM((sums_of, 4, width), F32),
    ]
    part = inner(here // 2, width)
    scratch += [block(), block(), block(4), block(3), block(), block(), part, part, block(), part]
    results = pl.pallas_call(
        functools.partial(layers_kernel, count, heads, group),
        out_shape=far + near,
        in_specs=[anywhere] * 8 + [inside] * 4,
        out_specs=[anywhere] * len(far) + [inside] * 2,
        scratch_shapes=scratch,
        compiler_params=pltpu.CompilerParams(
            collective_id=0, has_side_effects=True, vmem_limit_bytes=62 * 1024 * 1024
        ),
    )(*packs, *raw, *tables, owners[:, :, None], owners[:, None, :])
    return results[:2], results[2:6], results[-2:]


def unit_tiles(units, section, shared):
    tiles = units // 256
    first = section * units // 128 + shared * tiles
    return [(first + j) * 128 for j in range(tiles)], section * units + 256 * tiles + shared * 64


def pack_kernel(w_query, keyval, w_out, w_gate_up, w_down, qkv, out, gate_up, down):
    half = qkv.shape[2] - 2 * HEAD_SIZE
    units = w_down.shape[2] // 2
    for section in range(2):
        at = slice(section * half, (section + 1) * half)
        place = slice(section * HEAD_SIZE, (section + 1) * HEAD_SIZE)
        qkv[section, :, :half] = w_query[0, :, at]
        qkv[section, :, half:] = jnp.concatenate([keyval[0, :, 0, place], keyval[0, :, 1, place]], 1)
        out[section] = w_out[0, :, at]
        for shared in range(2):
            tiles, tail = unit_tiles(units, section, shared)
            for j, first in enumerate(tiles):
                for kind in range(2):
                    at = slice(256 * j + 128 * kind, 256 * j + 128 * kind + 128)
                    gate_up[section, shared, :, at] = w_gate_up[0, :, kind, first : first + 128]
                down[section, shared, :, 128 * j : 128 * j + 128] = w_down[0, :, first : first + 128]
            end = slice(tail, tail + 64)
            gate_up[section, shared, :, 256 * len(tiles) :] = jnp.concatenate(
                [w_gate_up[0, :, 0, end], w_gate_up[0, :, 1, end]], 1
            )
            some = w_down[0, :, end]
            down[section, shared, :, 128 * len(tiles) :] = jnp.concatenate(
                [some, jnp.zeros_like(some)], 1
            )


def unpack_kernel(qkv, out, gate_up, down, w_query, keyval, w_out, w_gate_up, w_down):
    half = qkv.shape[2] - 2 * HEAD_SIZE
    units = w_down.shape[2] // 2
    for section in range(2):
        at = slice(section * half, (section + 1) * half)
        w_query[0, :, at] = qkv[section, :, :half].astype(F32)
        w_out[0, :, at] = out[section].astype(F32)
        for shared in range(2):
            tiles, tail = unit_tiles(units, section, shared)
            for j, first in enumerate(tiles):
                for kind in range(2):
                    at = slice(256 * j + 128 * kind, 256 * j + 128 * kind + 128)
                    w_gate_up[0, :, kind, first : first + 128] = gate_up[section, shared, :, at].astype(F32)
                w_down[0, :, first : first + 128] = down[section, shared, :, 128 * j : 128 * j + 128].astype(F32)
        tiles, tail = unit_tiles(units, section, 0)
        last = slice(256 * len(tiles), 256 * len(tiles) + 128)
        both = [gate_up[section, shared, :, last].astype(F32) for shared in range(2)]
        w_gate_up[0, :, 0, tail : tail + 128] = jnp.concatenate([both[0][:, :64], both[1][:, :64]], 1)
        w_gate_up[0, :, 1, tail : tail + 128] = jnp.concatenate([both[0][:, 64:], both[1][:, 64:]], 1)
        at = slice(128 * len(tiles), 128 * len(tiles) + 64)
        w_down[0, :, tail : tail + 128] = jnp.concatenate(
            [down[section, shared, :, at].astype(F32) for shared in range(2)], 1
        )
    for kind in range(2):
        start = half + kind * HEAD_SIZE
        keyval[0, :, kind, :] = jnp.concatenate(
            [qkv[section, :, start : start + HEAD_SIZE].astype(F32) for section in range(2)], 1
        )


def row_specs(shapes, step):
    specs = []
    for dims, axis in shapes:
        block = tuple(step if i == axis else size for i, size in enumerate(dims))
        specs.append(
            pl.BlockSpec(block, functools.partial(lambda n, a, i: tuple(i if k == a else 0 for k in range(n)), len(dims), axis))
        )
    return specs


def packed(raw, kernel, outs, raw_first):
    rows = raw[0].shape[1] if raw_first else raw[0].shape[-2]
    step = min(rows, 64)
    wide = [(block.shape, 1) for block in (raw if raw_first else outs)]
    narrow = [(block.shape, len(block.shape) - 2) for block in (outs if raw_first else raw)]
    first, second = row_specs(wide, step), row_specs(narrow, step)
    return pl.pallas_call(
        kernel,
        grid=(rows // step,),
        out_shape=outs,
        in_specs=first if raw_first else second,
        out_specs=second if raw_first else first,
        compiler_params=pltpu.CompilerParams(vmem_limit_bytes=40 * 1024 * 1024),
    )(*raw)


def shards(
    layer_in,
    out_grad,
    doc_lengths,
    attn_gain,
    w_query,
    keyval_weight,
    w_out,
    mlp_gain,
    w_gate_up,
    w_down,
):
    micro, seqs, here, columns = layer_in.shape
    length = here * lax.axis_size("tensor")
    rows = w_query.shape[1]
    head_width = w_query.shape[2] // 2
    units = w_down.shape[2] // 4
    shape = jax.ShapeDtypeStruct
    raw = [w_query, keyval_weight, w_out, w_gate_up, w_down]
    packs = packed(
        raw,
        pack_kernel,
        [
            shape((2, rows, head_width + 2 * HEAD_SIZE), BF16),
            shape((2, rows, head_width), BF16),
            shape((2, 2, rows, 2 * units), BF16),
            shape((2, 2, rows, units + -units % 128), BF16),
        ],
        True,
    )
    owners = owners_of(doc_lengths.reshape(micro * seqs, -1), length)
    tables = rope_tables(length)
    (layer_out, in_grad), sums, (attn_term, mlp_term) = both_layers(
        packs, [layer_in, out_grad, attn_gain, mlp_gain], tables, owners
    )
    grads = packed(sums, unpack_kernel, [shape(block.shape, F32) for block in raw], False)
    grad_q, grad_kv, grad_o, grad_gu, grad_d = grads
    return layer_out, in_grad, attn_term, grad_q, grad_kv, grad_o, mlp_term, grad_gu, grad_d


def solution(mesh):
    activation = P(None, "dp", "tensor", "section")
    matrix = P("section", "dp", "tensor")
    stacked = P("section", "dp", None, "tensor")
    gain = P("section", None)
    return jax.shard_map(
        shards,
        mesh=mesh,
        in_specs=(
            activation,
            activation,
            P(None, "dp", None),
            gain,
            matrix,
            stacked,
            matrix,
            gain,
            stacked,
            matrix,
        ),
        out_specs=(
            activation,
            activation,
            gain,
            matrix,
            stacked,
            matrix,
            gain,
            stacked,
            matrix,
        ),
        check_vma=False,
    )
```

```python
import functools

import jax
import jax.numpy as jnp
from jax import lax
from jax.experimental import pallas as pl
from jax.experimental.pallas import tpu as pltpu
from jax.sharding import PartitionSpec as P

HEAD_SIZE = 64
NORM_EPSILON = 1e-05
ROPE_BASE = 10000.0
MASK_FILL = -1e30
FACTOR = HEAD_SIZE ** (-0.5)
BF16 = jnp.bfloat16
F32 = jnp.float32

def rope_tables(token_length):
    middle = HEAD_SIZE // 2
    frequency = ROPE_BASE ** (-(jnp.arange(middle, dtype=F32) * 2.0) / HEAD_SIZE)
    angles = frequency[:, None] * jnp.arange(token_length, dtype=F32)[None, :]
    return (
        jnp.concatenate([jnp.cos(angles), jnp.cos(angles)], 0),
        jnp.concatenate([jnp.sin(angles), jnp.sin(angles)], 0),
    )


def owners_of(lengths, token_length):
    bounds = jnp.cumsum(lengths, -1)
    places = jnp.arange(token_length, dtype=jnp.int32)
    return jnp.sum((places[None, :, None] >= bounds[:, None, :]).astype(jnp.int32), -1)


def visible_block(owner_col, owner_row):
    length = owner_col.shape[0]
    key_place = lax.broadcasted_iota(jnp.int32, (length, length), 0)
    query_place = lax.broadcasted_iota(jnp.int32, (length, length), 1)
    return (owner_col == owner_row) & (key_place <= query_place)


def rope(u, cosine, sine):
    half = HEAD_SIZE // 2
    return u * cosine + jnp.concatenate([-u[half:], u[:half]], 0) * sine


def rope_back(u, cosine, sine):
    half = HEAD_SIZE // 2
    w = u * sine
    return u * cosine + jnp.concatenate([w[half:], -w[:half]], 0)


def normed(values, gain):
    inverse = lax.rsqrt(jnp.mean(values * values, -1, keepdims=True) + NORM_EPSILON)
    return (values * inverse * gain).astype(BF16)


def norm_back(grad, values, gain):
    inverse = lax.rsqrt(jnp.mean(values * values, -1, keepdims=True) + NORM_EPSILON)
    scaled = values * inverse
    gained = grad * gain
    into = inverse * (gained - scaled * jnp.mean(gained * scaled, -1, keepdims=True))
    return into, jnp.sum(grad * scaled, 0, keepdims=True)


def crossed(values, group):
    count = values.shape[-1] // group
    return jnp.concatenate(
        [values[:, (g ^ 1) * group : ((g ^ 1) + 1) * group] for g in range(count)], 1
    )


def reordered(values, count):
    me = lax.axis_index("dp")
    group = values.shape[-1] // count
    while group < values.shape[-1]:
        values = jnp.where(lax.rem(me, 2) == 1, crossed(values, group), values)
        me, group = me // 2, group * 2
    return values


def dot_t(left, right):
    return lax.dot_general(left, right, (((1,), (1,)), ((), ())), preferred_element_type=F32)


def dot_n(left, right):
    return jnp.dot(left, right, preferred_element_type=F32)


def dot_tn(left, right):
    return lax.dot_general(left, right, (((0,), (0,)), ((), ())), preferred_element_type=F32)


class Hops:
    def __init__(self, send, recv):
        self.send, self.recv, self.count, self.started = send, recv, 0, []
        self.index = {name: lax.axis_index(name) for name in ("section", "dp", "tensor")}
        self.other = 1 - self.index["section"]

    def to(self, offset):
        dp = self.index["dp"]
        for bit in range(offset.bit_length()):
            if offset >> bit & 1:
                low = lax.rem(dp // (1 << bit), 2)
                dp = dp + (1 - 2 * low) * (1 << bit)
        return (self.index["section"], dp, self.index["tensor"])

    def across(self):
        return (self.other, self.index["dp"], self.index["tensor"])

    def core(self):
        return (self.index["section"], self.index["dp"], 1 - self.index["tensor"])

    def at(self, source, target, device, index):
        return pltpu.make_async_remote_copy(
            src_ref=source,
            dst_ref=target,
            send_sem=self.send.at[index],
            recv_sem=self.recv.at[index],
            device_id=device,
            device_id_type=pl.DeviceIdType.MESH,
        )

    def claim(self, number=1):
        self.count += number
        return self.count - number

    def start(self, source, target, device):
        copy = self.at(source, target, device, self.claim())
        copy.start()
        self.started.append(copy)
        return copy

    def start_either(self, choice, first, second, target, device):
        index = self.claim()
        copy = self.at(first, target, device, index)
        backup = self.at(second, target, device, index)
        pl.when(choice)(copy.start)
        pl.when(jnp.logical_not(choice))(backup.start)
        self.started.append(copy)
        return copy

    def sent(self, copies):
        copies = list(copies)
        for copy in copies:
            copy.wait_send()
        gone = {id(copy) for copy in copies}
        self.started = [copy for copy in self.started if id(copy) not in gone]

    def greet(self, offsets):
        barrier = pltpu.get_barrier_semaphore()
        devices = [self.to(offset) for offset in offsets] + [self.across(), self.core()]
        for device in devices:
            pl.semaphore_signal(
                barrier, inc=1, device_id=device, device_id_type=pl.DeviceIdType.MESH
            )
        pl.semaphore_wait(barrier, len(devices))

    def drain(self):
        for copy in self.started:
            copy.wait_send()


class Local:
    AT_ONCE = 6

    def __init__(self, sems):
        self.sems, self.count = sems, self.AT_ONCE

    def claim(self, number=1):
        self.count += number
        return self.count - number

    def make(self, source, target):
        return pltpu.make_async_copy(source, target, self.sems.at[self.claim()])

    def start(self, source, target):
        copy = self.make(source, target)
        copy.start()
        return copy

    def now(self, *moves):
        waits = []
        for index, move in enumerate(moves):
            make = lambda source: pltpu.make_async_copy(source, move[-1], self.sems.at[index])
            copy = make(move[-2])
            if len(move) == 2:
                copy.start()
            else:
                pl.when(move[0])(make(move[1]).start)
                pl.when(jnp.logical_not(move[0]))(copy.start)
            waits.append(copy)
        for copy in waits:
            copy.wait()


def reached(count):
    return [1] + [2 * k for k in range(1, count // 2)]


class Spread:
    def __init__(self, hops, local, own, turned, group):
        self.hops, self.local, self.own, self.turned, self.group = hops, local, own, turned, group

    def four(self, rows, slots):
        hops, own = self.hops, self.own
        section, tensor = hops.index["section"], hops.index["tensor"]
        own[...] = rows
        slot = 2 * section + tensor
        self.over_y = hops.start(own, slots.at[slot], hops.across())
        self.over_core = hops.start(own, slots.at[slot], hops.core())
        self.keep = self.local.start(own, slots.at[slot])

    def four_end(self, slots):
        hops = self.hops
        self.over_y.wait_recv()
        across = 2 * (1 - hops.index["section"]) + hops.index["tensor"]
        last = hops.start(slots.at[across], slots.at[across], hops.core())
        self.over_core.wait_recv()
        last.wait_recv()
        self.keep.wait()
        hops.sent([self.over_y, self.over_core, last])

    def halves(self):
        half = self.own.shape[0] // 2
        return pl.ds(0, half), pl.ds(half, half)

    def eight(self, rows, slots):
        hops, own, turned = self.hops, self.own, self.turned
        own[...] = rows
        turned[...] = crossed(rows, self.group)
        lo, hi = self.halves()
        y, z, core = hops.across(), hops.to(2), hops.core()
        self.over = [
            hops.start(own.at[hi], slots.at[2, hi], y),
            hops.start(turned.at[lo], slots.at[4, lo], z),
            hops.start(own.at[lo], slots.at[2, lo], y),
            hops.start(turned.at[hi], slots.at[4, hi], z),
        ]
        self.cores = [hops.start(own, slots.at[1], core)]
        self.keep = self.local.start(own, slots.at[0])

    def eight_middle(self, slots):
        hops, group = self.hops, self.group
        lo, hi = self.halves()
        self.over[0].wait_recv()
        self.diag = [
            hops.start(
                slots.at[2, hi, pl.ds(g * group, group)],
                slots.at[6, hi, pl.ds((g ^ 1) * group, group)],
                hops.to(2),
            )
            for g in range(self.own.shape[1] // group)
        ]
        self.over[1].wait_recv()
        self.diag.append(hops.start(slots.at[4, lo], slots.at[6, lo], hops.across()))

    def eight_end(self, slots):
        hops = self.hops
        core = hops.core()
        self.over[2].wait_recv()
        self.cores.append(hops.start(slots.at[2], slots.at[3], core))
        self.over[3].wait_recv()
        self.cores.append(hops.start(slots.at[4], slots.at[5], core))
        for copy in self.diag:
            copy.wait_recv()
        self.cores.append(hops.start(slots.at[6], slots.at[7], core))
        for copy in self.cores:
            copy.wait_recv()
        self.keep.wait()
        hops.sent(self.over + self.diag + self.cores)


class Sums:
    def __init__(self, hops, partial, core, out, from_y, from_z, part_y, part_z, group):
        self.hops, self.partial, self.core, self.out, self.group = hops, partial, core, out, group
        self.from_y, self.from_z, self.part_y, self.part_z = from_y, from_z, part_y, part_z

    def four(self):
        hops, core, out, from_y, partial = self.hops, self.core, self.out, self.from_y, self.partial
        section, tensor = hops.index["section"], hops.index["tensor"]
        slots = [2 * section, 2 * (1 - section)]
        far = {
            c: hops.start(partial.at[slots[c] + 1 - tensor], core.at[c], hops.core()) for c in (1, 0)
        }
        far[1].wait_recv()
        out[0] = (partial[slots[1] + tensor].astype(F32) + core[1].astype(F32)).astype(BF16)
        over_y = hops.start(out.at[0], from_y, hops.across())
        far[0].wait_recv()
        over_y.wait_recv()
        total = (
            partial[slots[0] + tensor].astype(F32) + core[0].astype(F32) + from_y[...].astype(F32)
        )
        hops.sent([far[0], far[1], over_y])
        return total

    def halves(self):
        half = self.out.shape[1] // 2
        return pl.ds(0, half), pl.ds(half, half)

    def added(self, c, rows):
        return self.partial[2 * c, rows, :].astype(F32) + self.core[c, rows, :].astype(F32)

    def eight(self):
        hops, out, group = self.hops, self.out, self.group
        lo, hi = self.halves()
        y, z = hops.across(), hops.to(2)
        self.far = {
            c: hops.start(self.partial.at[2 * c + 1], self.core.at[c], hops.core())
            for c in (3, 1, 2, 0)
        }
        self.far[3].wait_recv()
        out[2, lo, :] = self.added(3, lo).astype(BF16)
        self.diag_y = hops.start(out.at[2, lo], self.part_y, y)
        out[2, hi, :] = crossed(self.added(3, hi), group).astype(BF16)
        self.diag_z = hops.start(out.at[2, hi], self.part_z, z)
        self.far[1].wait_recv()
        out[0, lo, :] = self.added(1, lo).astype(BF16)
        self.over = [hops.start(out.at[0, lo], self.from_y.at[lo], y)]
        self.far[2].wait_recv()
        out[1, hi, :] = crossed(self.added(2, hi), group).astype(BF16)
        self.over.append(hops.start(out.at[1, hi], self.from_z.at[hi], z))

    def eight_middle(self):
        hops, out, group = self.hops, self.out, self.group
        lo, hi = self.halves()
        self.diag_y.wait_recv()
        out[1, lo, :] = crossed(self.added(2, lo) + self.part_y[...].astype(F32), group).astype(BF16)
        self.over.append(hops.start(out.at[1, lo], self.from_z.at[lo], hops.to(2)))
        self.diag_z.wait_recv()
        out[0, hi, :] = (self.added(1, hi) + self.part_z[...].astype(F32)).astype(BF16)
        self.over.append(hops.start(out.at[0, hi], self.from_y.at[hi], hops.across()))

    def eight_end(self):
        self.far[0].wait_recv()
        for copy in self.over:
            copy.wait_recv()
        total = (
            self.partial[0].astype(F32)
            + self.core[0].astype(F32)
            + self.from_y[...].astype(F32)
            + self.from_z[...].astype(F32)
        )
        self.hops.sent(list(self.far.values()) + [self.diag_y, self.diag_z] + self.over)
        return total


QKV, OUT, GU, DOWN = range(4)
IS_SHARED = (False, False, True, True)


def others(k, kinds):
    return [k] + (list(range(4, kinds)) if k == 1 else [])


class Gather:
    def __init__(self, hops, local, count, packs, crossed_over, full):
        self.hops, self.local, self.packs, self.over, self.full = hops, local, packs, crossed_over, full
        self.kinds = count // 2
        self.arrived, self.have = {}, set()
        self.half = lax.rem(hops.index["dp"] // 2, 2)
        self.rows = packs[0].shape[-2]

    def cross(self, a):
        hops = self.hops
        self.arrived[a] = hops.start(self.packs[a].at[hops.other], self.over[a], hops.across())

    def block(self, a, layer, r):
        return self.full[layer][a].at[pl.ds(r * self.rows, self.rows)]

    def source(self, a, other):
        if a not in self.have:
            self.have.add(a)
            self.arrived[a].wait_recv()
        section = self.hops.index["section"]
        if not IS_SHARED[a]:
            return self.packs[a].at[section], self.over[a]
        which = 1 - self.half if other else self.half
        return self.packs[a].at[section, which], self.over[a].at[which]

    def straight(self, a, layer):
        first, second = self.source(a, False)
        here = self.hops.index["section"] == layer
        self.arrived[a, layer, "x", 0] = self.hops.start_either(
            here, first, second, self.block(a, layer, 1), self.hops.to(1)
        )

    def begin(self, a, layer, step):
        for k in others(step, self.kinds):
            if IS_SHARED[a] or k == 1 or k % 2 == 0:
                first, second = self.source(a, k % 2 == 1)
                self.arrived[a, layer, k] = self.hops.start_either(
                    self.hops.index["section"] == layer,
                    first,
                    second,
                    self.block(a, layer, 2 * k),
                    self.hops.to(2 * k),
                )

    def onward(self, a, layer, step):
        hops = self.hops
        for k in others(step, self.kinds):
            self.arrived[a, layer, k].wait_recv()
            self.arrived[a, layer, "x", k] = hops.start(
                self.block(a, layer, 2 * k), self.block(a, layer, 2 * k + 1), hops.to(1)
            )
            if not IS_SHARED[a] and k % 2 == 0:
                self.arrived[a, layer, k + 1] = hops.start(
                    self.block(a, layer, 2 * k), self.block(a, layer, 2 * k + 2), hops.to(2)
                )

    def complete(self, a, layer):
        for k in range(self.kinds):
            self.arrived[a, layer, "x", k].wait_recv()

    def parts(self, a, layer, target):
        first, second = self.source(a, False)
        rest = pl.ds(self.rows, target.shape[0] - self.rows)
        here = self.hops.index["section"] == layer
        return [
            (here, first, second, target.at[pl.ds(0, self.rows)]),
            (self.full[layer][a].at[rest], target.at[rest]),
        ]


def attention_step(heads, qkv, place, cos, sin, visible, rotated, log_total):
    width = heads * HEAD_SIZE
    keys = rope(qkv[width : width + HEAD_SIZE, place], cos, sin).astype(BF16)
    values = qkv[width + HEAD_SIZE :, place].astype(BF16)
    rotated[width : width + HEAD_SIZE, place] = keys
    rotated[width + HEAD_SIZE :, place] = values
    attended = []
    for h in range(heads):
        at = slice(h * HEAD_SIZE, (h + 1) * HEAD_SIZE)
        queries = rope(qkv[at, place], cos, sin).astype(BF16)
        rotated[at, place] = queries
        score = dot_tn(keys, queries)
        score = jnp.where(visible, score * FACTOR, MASK_FILL)
        top = jnp.max(score, 0, keepdims=True)
        exponent = jnp.exp(score - top)
        total = jnp.sum(exponent, 0, keepdims=True)
        prob = (exponent * (1.0 / total)).astype(BF16)
        attended.append(dot_n(values, prob))
        log_total[h : h + 1, place] = top + jnp.log(total)
    return jnp.concatenate(attended, 0).T.astype(BF16)


def attention_back_step(heads, rotated, grad_att, place, cos, sin, visible, log_total):
    width = heads * HEAD_SIZE
    keys = rotated[width : width + HEAD_SIZE, place]
    values = rotated[width + HEAD_SIZE :, place]
    length = keys.shape[1]
    grad_keys = jnp.zeros((HEAD_SIZE, length), F32)
    grad_values = jnp.zeros((HEAD_SIZE, length), F32)
    found = []
    for h in range(heads):
        at = slice(h * HEAD_SIZE, (h + 1) * HEAD_SIZE)
        queries = rotated[at, place]
        grad = grad_att[at, :]
        score = jnp.where(visible, dot_tn(keys, queries) * FACTOR, MASK_FILL)
        prob = jnp.exp(score - log_total[h : h + 1, place])
        grad_prob = dot_tn(values, grad)
        inner = jnp.sum(prob * grad_prob, 0, keepdims=True)
        grad_score = (FACTOR * prob * (grad_prob - inner)).astype(BF16)
        found.append(rope_back(dot_n(keys, grad_score), cos, sin))
        grad_keys += dot_t(queries, grad_score)
        grad_values += dot_t(grad, prob.astype(BF16))
    found += [rope_back(grad_keys, cos, sin), grad_values]
    return jnp.concatenate(found, 0).T.astype(BF16)


def steps_of(names):
    found = []
    for name in names:
        letters = name.rstrip("0123456789")
        found.append((letters, *(int(digit) for digit in name[len(letters) :])))
    return found


ORDER = (
    "c0", "B002", "B001", "c1", "B012", "X01", "B102", "c2", "n0", "X00", "O001", "B101",
    "O002", "X20", "B202", "O003", "B201", "m0", "X11", "B111", "c3", "O202", "O102", "B301",
    "B011", "B303", "B203", "B312", "a0", "O101", "O103", "X10", "O201", "B112", "e0", "q0",
    "O303", "O011", "r0", "O301", "X30", "g0", "n1", "h0", "O203", "B302", "m1", "O012",
    "i0", "O112", "O302", "B212", "u0", "d0", "O113", "s0", "O111", "t0", "B211", "B311",
    "B213", "O013", "O212", "v0", "B313", "a1", "X31", "e1", "O211", "X21", "q1", "r1",
    "O213", "g1", "h1", "O311", "i1", "O313", "g2", "O312", "u1", "h2", "i2", "bl1",
    "S31", "bk1", "bp1", "E31", "bs1", "S21", "bt1", "E21", "Z311", "bv1", "ba1", "Z313",
    "be1", "bq1", "Z211", "Z312", "br1", "S11", "bg1", "bh1", "Z210", "Z213", "E11", "Z212",
    "E01", "Z310", "Y31", "S01", "bi1", "bl0", "bk0", "S30", "E30", "bp0", "bs0", "Z113",
    "Y21", "Z302", "Z013", "bt0", "Z111", "S20", "Z110", "Z011", "E20", "Z200", "Z303", "Z012",
    "bv0", "ba0", "Z112", "be0", "Z010", "Z201", "Z301", "Y01", "Z203", "Y11", "bq0", "Z202",
    "Z300", "E00", "S00", "E10", "br0", "bn0", "Y30", "bn1", "d1", "Z003", "bn2", "s1",
    "S10", "Z000", "Y20", "Z002", "Z103", "Z001", "Z101", "Z102", "Z100", "t1", "Y00", "Y10",
    "bn3", "w1", "bn4", "v1", "bn5", "w0",
)


def into_partial(block, w, partial, here, width, tile):
    @pl.loop(0, width // tile)
    def _(n):
        cut = pl.ds(pl.multiple_of(n * tile, tile), tile)
        some = dot_t(block[...], w[cut, :])
        partial[:, :, cut] = some.astype(BF16).reshape(partial.shape[0], here, tile)


def add_rows(target, left, right):
    rows = target.shape[0]
    step = min(32, rows)

    @pl.loop(0, rows // step)
    def _(i):
        at = pl.ds(pl.multiple_of(i * step, step), step)
        target[at, :] = (left[at, :].astype(F32) + right[at, :].astype(F32)).astype(BF16)


class Scatter:
    def __init__(self, hops, local, kept, staged, landed, distant, sums_out, one_block, term, rows):
        self.hops, self.local, self.kept, self.staged = hops, local, kept, staged
        self.landed, self.distant, self.sums_out = landed, distant, sums_out
        self.one_block, self.term, self.rows = one_block, term, rows
        self.kinds = kept[0].shape[0]
        self.half = lax.rem(hops.index["dp"] // 2, 2)
        self.section = hops.index["section"]
        self.copies, self.ending = {}, []

    def renew(self, a):
        assert (a, 1) in [entry[:2] for entry in self.ending]
        out = [self.copies[a, 1, "z", k] for k in range(1, self.kinds)]
        self.hops.sent([copy for copy in out if copy is not None])
        for b, layer, keep, away in self.ending:
            if (b, layer) == (a, 1):
                pl.when(self.section == layer)(keep.wait)
                pl.when(self.section != layer)(away.wait_send)

    def stage(self, a, layer):
        hops, local, rows, kept = self.hops, self.local, self.rows, self.kept
        if layer == 0 and rows % 128:
            self.renew(a)
        base, at = hops.claim(self.kinds), local.claim(self.kinds)
        cols = pl.ds(0, kept[a].shape[-1])
        source, target = self.staged[layer][a], self.landed[layer][a]

        @pl.loop(0, self.kinds)
        def _(k):
            if rows % 128:
                both = self.term(a, 2 * k, 2 * rows)
                self.one_block[:, cols] = both[rows:]
                kept[a][k] = both[:rows]
            else:
                self.one_block[:, cols] = self.term(a, 2 * k + 1, rows)
            keep = pltpu.make_async_copy(
                self.one_block.at[:, cols], source.at[k], local.sems.at[at + k]
            )
            keep.start()
            keep.wait()
            hops.at(source.at[k], target.at[k], hops.to(1), base + k).start()

        for k in range(self.kinds):
            copy = hops.at(source.at[k], target.at[k], hops.to(1), base + k)
            self.copies[a, layer, "x", k] = copy
            hops.started.append(copy)

    def evens(self, a, layer):
        if self.rows % 128:
            return
        if layer == 0:
            self.renew(a)

        @pl.loop(0, self.kinds)
        def _(k):
            self.kept[a][k] = self.term(a, 2 * k, self.rows)

    def fetch(self, a, source):
        block = self.one_block.at[:, pl.ds(0, self.kept[a].shape[-1])]
        self.local.now((source, block))
        return block

    def meet(self, a, layer, step):
        hops, kept, copies = self.hops, self.kept[a], self.copies
        far = self.distant[layer][a]
        steps = [0] if step == 0 else list(reversed(others(step, self.kinds)))
        for k in steps:
            copies[a, layer, "x", k].wait_recv()
            add_rows(kept.at[k], kept.at[k], self.fetch(a, self.landed[layer][a].at[k]))
            if not IS_SHARED[a] and k % 2 == 0 and k:
                copies[a, layer, "z", k + 1].wait_recv()
                add_rows(kept.at[k], kept.at[k], self.fetch(a, far.at[k + 1]))
            if k:
                passed = not IS_SHARED[a] and k % 2 == 1 and k > 1
                copies[a, layer, "z", k] = hops.start(
                    kept.at[k], far.at[k], hops.to(2 if passed else 2 * k)
                )

    def deliver(self, a, layer):
        hops, kept, copies = self.hops, self.kept[a], self.copies
        far = self.distant[layer][a]
        mine, other = [], []
        for k in range(1, self.kinds):
            if IS_SHARED[a] or k == 1 or k % 2 == 0:
                copies[a, layer, "z", k].wait_recv()
                (other if IS_SHARED[a] and k % 2 else mine).append(k)
        for k in mine:
            add_rows(kept.at[0], kept.at[0], self.fetch(a, far.at[k]))
        pieces = [kept.at[0]]
        if IS_SHARED[a]:
            hops.sent([copies[a, layer, "z", 1]])
            copies[a, layer, "z", 1] = None
            self.local.now((far.at[other[0]], kept.at[1]))
            for k in other[1:]:
                add_rows(kept.at[1], kept.at[1], self.fetch(a, far.at[k]))
            pieces.append(kept.at[1])
        for number, piece in enumerate(pieces):
            which = self.half if number == 0 else 1 - self.half
            target = self.sums_out[a].at[self.section]
            if IS_SHARED[a]:
                target = self.sums_out[a].at[self.section, which]
            keep = self.local.make(piece, target)
            away = hops.at(piece, target, hops.across(), hops.claim())
            pl.when(self.section == layer)(keep.start)
            pl.when(self.section != layer)(away.start)
            self.ending.append((a, layer, keep, away))

    def end(self):
        for a, layer, keep, away in self.ending:
            pl.when(self.section == layer)(away.wait_recv)
            if layer == 0:
                pl.when(self.section == layer)(keep.wait)
                pl.when(self.section != layer)(away.wait_send)


def layers_kernel(count, heads, group, *refs):
    refs = list(refs)
    take = lambda number: [refs.pop(0) for _ in range(number)]
    packs, raw_rows, raw_gains = take(4), take(2), take(2)
    cosine, sine, owner_col, owner_row = take(4)
    ends, sums_out = take(2), take(4)
    crossed_over, full = take(4), (take(4), take(4))
    rows_attn_out, hidden_out, (rows_mlp_out, gate_up_out, grad_out) = take(2), take(2), take(3)
    staged, landed, distant = [(take(4), take(4)) for _ in range(3)]
    gain_sums = take(2)
    send, recv, sems = take(3)
    w_low, w_out, w_gu = take(3)
    slots4, slots8, partial, rows_mlp = take(4)
    qkv, gate_up, hidden = take(3)
    rotated, attended, log_total, middles = [take(2) for _ in range(4)]
    grad_att, grad_qkv = take(2)
    kept, (one_block,) = take(4), take(1)
    entering, handed, grad_middle = take(3)
    raw_whole, cotangent, through = take(3)
    gain_whole, gains, gain_terms, gain_landed = take(4)
    own, turned, core, out, from_y, from_z, part_y, part_z, last_z, last_part = take(10)
    hops, local = Hops(send, recv), Local(sems)
    hops.greet(reached(count))
    spread = Spread(hops, local, own, turned, group)
    sums = Sums(hops, partial, core, out, from_y, from_z, part_y, part_z, group)
    sums_last = Sums(hops, partial, core, out, from_y, last_z, part_y, last_part, group)
    gather = Gather(hops, local, count, packs, crossed_over, full)
    section = hops.index["section"]
    here, width = own.shape
    rows = width // count
    length = cosine.shape[1]
    seqs = slots4.shape[0] * here // length
    per_seq = length // here
    tile = 512
    units = hidden.shape[1]
    real = gate_up.shape[1] // 2
    whole = real // 128
    rest = real - whole * 128
    split = rotated[0].shape[0]
    rows_attn = partial.at[pl.ds(4, 4)]
    stores = []

    def store(source, target):
        stores.append(local.start(source, target))

    def settle():
        for copy in stores:
            copy.wait()
        stores.clear()

    def span(i, size):
        return pl.ds(pl.multiple_of(i * size, size), size)

    w_qkv = w_low.at[:, pl.ds(0, split)]

    def project(layer):
        gather.complete(QKV, layer)
        gather.complete(OUT, layer)
        local.now(*gather.parts(QKV, layer, w_qkv), *gather.parts(OUT, layer, w_out))

        @pl.loop(0, seqs)
        def _(i):
            block = slots4[pl.ds(i * per_seq, per_seq)].reshape(length, width)
            place = span(i, length)
            qkv[:, place] = dot_n(block, w_low[:, :split]).T
            visible = visible_block(owner_col[i], owner_row[i])
            attended[layer][place, :] = attention_step(
                heads, qkv, place, cosine[...], sine[...], visible, rotated[layer], log_total[layer]
            )

        store(slots4, rows_attn_out[layer])

        @pl.loop(0, width // tile)
        def _(n):
            cut = span(n, tile)
            for i in range(seqs):
                some = dot_t(attended[layer][i * length : (i + 1) * length, :], w_out[cut, :])
                partial[i * per_seq : (i + 1) * per_seq, :, cut] = some.astype(BF16).reshape(
                    per_seq, here, tile
                )

    def expand(layer):
        gather.complete(GU, layer)
        local.now(*gather.parts(GU, layer, w_gu))

        block = slots8[...].reshape(slots8.shape[0] * here, width)

        @pl.loop(0, whole)
        def _(n):
            cut = span(n, 256)
            both = dot_n(block, w_gu[:, cut])
            gate_up[:, cut] = both.astype(BF16)
            gate, up = both[:, :128], both[:, 128:]
            hidden[:, span(n, 128)] = (gate * jax.nn.sigmoid(gate) * up).astype(BF16)

        if rest:
            both = dot_n(block, w_gu[:, whole * 256 :])
            gate_up[:, whole * 256 :] = both.astype(BF16)
            gate, up = both[:, :rest], both[:, rest:]
            some = (gate * jax.nn.sigmoid(gate) * up).astype(BF16)
            hidden[:, whole * 128 :] = jnp.concatenate([some, jnp.zeros_like(some)], 1)

        if layer == 0:
            store(slots8, rows_mlp_out)
            store(gate_up, gate_up_out)
        else:
            rows_mlp[...] = slots8[...]
        store(hidden, hidden_out[layer])

    def entry(layer):
        return entering if layer == 0 else handed

    waiting = {}

    def bring(number):
        target = raw_whole.at[:, span(section, width // 2)]
        waiting[number] = [
            hops.start(raw_rows[number].at[hops.other, 0], target, hops.across()),
            local.start(raw_rows[number].at[section, 0], target),
        ]
        if number == 0:
            for kind in range(2):
                waiting[number] += [
                    hops.start(raw_gains[kind], gain_whole.at[section, kind], hops.across()),
                    local.start(raw_gains[kind], gain_whole.at[section, kind]),
                ]

    def brought(number):
        for place, copy in enumerate(waiting[number]):
            copy.wait() if place % 2 else copy.wait_recv()
        rows_here = reordered(raw_whole[...].astype(F32), count)
        if number == 0:
            entering[...] = rows_here
            for layer in range(2):
                for kind in range(2):
                    mark = 2 * layer + kind
                    gains[mark : mark + 1, :] = reordered(gain_whole[layer, kind], count)
        else:
            cotangent[...] = rows_here.astype(BF16)

    def gain(layer, kind):
        mark = 2 * layer + kind
        return gains[mark : mark + 1, :]

    def ready(layer):
        settle()
        if layer == 1:
            local.now((grad_out, slots8))
        else:
            local.now((gate_up_out, gate_up), (hidden_out[0], hidden), (rows_mlp_out, rows_mlp))

    def widen(layer):
        if layer == 1:
            gather.complete(DOWN, 1)
        local.now(*gather.parts(DOWN, layer, w_low))

        @pl.loop(0, slots8.shape[0] // 2)
        def _(c):
            block = slots8[pl.ds(c * 2, 2)].reshape(2 * here, width)
            place = span(c, 2 * here)
            grad_hidden = dot_n(block, w_low[...]).astype(BF16).astype(F32)

            def back(grad, gate, up):
                gate, up = gate.astype(F32), up.astype(F32)
                sig = jax.nn.sigmoid(gate)
                return [
                    (grad * up * sig * (1.0 + gate * (1.0 - sig))).astype(BF16),
                    (grad * (gate * sig)).astype(BF16),
                ]

            for n in range(whole):
                at = slice(n * 256, n * 256 + 256)
                both = gate_up[place, at]
                gate_up[place, at] = jnp.concatenate(
                    back(grad_hidden[:, n * 128 : n * 128 + 128], both[:, :128], both[:, 128:]), 1
                )
            if rest:
                both = gate_up[place, whole * 256 :]
                gate_up[place, whole * 256 :] = jnp.concatenate(
                    back(grad_hidden[:, whole * 128 : real], both[:, :rest], both[:, rest:]), 1
                )

    def attend(layer):
        local.now(
            *gather.parts(OUT, layer, w_out),
            *gather.parts(QKV, layer, w_qkv),
            (rows_attn_out[layer], rows_attn),
        )

        @pl.loop(0, seqs)
        def _(i):
            block = slots4[pl.ds(i * per_seq, per_seq)].reshape(length, width)
            place = span(i, length)
            grad_att[...] = dot_n(block, w_out[...]).T.astype(BF16)
            visible = visible_block(owner_col[i], owner_row[i])
            grad_qkv[place, :] = attention_back_step(
                heads, rotated[layer], grad_att, place, cosine[...], sine[...], visible, log_total[layer]
            )

        @pl.loop(0, width // tile)
        def _(n):
            cut = span(n, tile)
            for i in range(seqs):
                some = dot_t(grad_qkv[i * length : (i + 1) * length, :], w_low[cut, :split])
                partial[i * per_seq : (i + 1) * per_seq, :, cut] = some.astype(BF16).reshape(
                    per_seq, here, tile
                )

    working = [1]

    def term(a, r, size):
        slots, right = {
            QKV: (rows_attn, grad_qkv),
            OUT: (slots4, attended[working[0]]),
            GU: (rows_mlp, gate_up),
            DOWN: (slots8, hidden),
        }[a]
        cut = pl.ds(pl.multiple_of(r * rows, max(rows, 128)), size)
        return dot_tn(slots[:, :, cut].reshape(slots.shape[0] * here, size), right[...]).astype(BF16)

    scatter = Scatter(
        hops, local, kept, staged, landed, distant, sums_out, one_block, term, rows
    )

    def back_through(total, source, values, layer, kind, result):
        into, term_row = norm_back(total, values, gain(layer, kind))
        mark = 2 * layer + kind
        gain_terms[0, mark : mark + 1, :] = term_row
        result[...] = (source + into).astype(result.dtype)

    leaving = []

    def leave(number, block):
        block[...] = reordered(block[...].astype(F32), count).astype(BF16)
        target = ends[number].at[section, 0]
        leaving.append(local.start(block.at[:, span(section, width // 2)], target))
        leaving.append(hops.start(block.at[:, span(hops.other, width // 2)], target, hops.across()))

    gain_places, offset = [hops.core(), hops.across()], 1
    while offset < count:
        gain_places.append(hops.to(offset))
        offset *= 2
    gain_moves = []

    def add_gains(step):
        for number in range(step, len(gain_places) + 1) if step == 5 else [step]:
            if number == 0:
                gain_terms[0] = reordered(gain_terms[0], count)
            else:
                gain_moves[-1].wait_recv()
                gain_terms[number] = gain_terms[number - 1] + gain_landed[number - 1]
            if number < len(gain_places):
                gain_moves.append(
                    hops.start(gain_terms.at[number], gain_landed.at[number], gain_places[number])
                )
        if step == 5:
            total = gain_terms[len(gain_places)]
            mine = jnp.where(section == 0, total[0:2], total[2:4])
            for kind in range(2):
                gain_sums[kind][...] = mine[kind : kind + 1]

    for name, *at in steps_of(ORDER):
        layer = at[0]
        if name == "c":
            gather.cross(*at)
        elif name == "X":
            gather.straight(*at)
        elif name == "B":
            gather.begin(*at)
        elif name == "O":
            gather.onward(*at)
        elif name == "n":
            bring(*at)
        elif name == "m":
            brought(*at)
        elif name == "a":
            spread.four(normed(entry(layer)[...], gain(layer, 0)), slots4)
        elif name in ("e", "be"):
            spread.four_end(slots4)
        elif name == "q":
            project(layer)
        elif name == "r":
            middles[layer][...] = entry(layer)[...] + sums.four()
        elif name == "g":
            if layer == 2:
                spread.eight(cotangent[...], grad_out)
            else:
                spread.eight(normed(middles[layer][...], gain(layer, 1)), slots8)
        elif name == "h":
            spread.eight_middle(grad_out if layer == 2 else slots8)
        elif name == "i":
            spread.eight_end(grad_out if layer == 2 else slots8)
        elif name == "u":
            expand(layer)
        elif name == "d":
            if layer == 0:
                gather.complete(DOWN, 0)
            else:
                local.now((hidden_out[1], hidden))
            local.now(*gather.parts(DOWN, layer, w_low))
            into_partial(hidden, w_low, partial, here, width, tile // 2)
        elif name == "s":
            settle()
            (sums_last if layer == 1 else sums).eight()
        elif name == "t":
            (sums_last if layer == 1 else sums).eight_middle()
        elif name == "v":
            if layer == 1:
                raw_whole[...] = (middles[1][...] + sums_last.eight_end()).astype(BF16)
            else:
                handed[...] = (middles[0][...] + sums.eight_end()).astype(BF16).astype(F32)
        elif name == "bl":
            working[0] = layer
            ready(layer)
        elif name == "bk":
            widen(layer)
        elif name == "S":
            scatter.stage(*at)
        elif name == "E":
            scatter.evens(*at)
        elif name == "Z":
            scatter.meet(*at)
        elif name == "Y":
            scatter.deliver(*at)
        elif name == "bp":
            if layer == 0:
                local.now(*gather.parts(GU, 0, w_gu))
            into_partial(gate_up, w_gu, partial, here, width, tile // 2)
        elif name == "bs":
            sums.eight()
        elif name == "bt":
            sums.eight_middle()
        elif name == "bv":
            total = sums.eight_end()
            source = (cotangent if layer == 1 else through)[...].astype(F32)
            back_through(total, source, middles[layer][...], layer, 1, grad_middle)
        elif name == "ba":
            spread.four(grad_middle[...].astype(BF16), slots4)
        elif name == "bq":
            attend(layer)
        elif name == "br":
            back_through(sums.four(), grad_middle[...], entry(layer)[...], layer, 0, through)
        elif name == "bg":
            spread.eight(through[...], slots8)
        elif name == "bh":
            spread.eight_middle(slots8)
        elif name == "bi":
            spread.eight_end(slots8)
        elif name == "w":
            leave(layer, (raw_whole, through)[layer])
        elif name == "bn":
            add_gains(layer)
    scatter.end()
    settle()
    for place, copy in enumerate(leaving):
        copy.wait_recv() if place % 2 else copy.wait()
    hops.drain()


def both_layers(packs, raw, tables, owners):
    count = lax.axis_size("dp")
    kinds = count // 2
    anywhere = pl.BlockSpec(memory_space=pl.ANY)
    inside = pl.BlockSpec(memory_space=pltpu.VMEM)
    seqs, length = owners.shape
    tokens = seqs * length
    here, width = tokens // 4, packs[0].shape[-2] * count
    rows = width // count
    columns = [pack.shape[-1] for pack in packs]
    head_width = columns[OUT]
    heads = head_width // HEAD_SIZE
    group = 2 * width // count
    shape = lambda *dims: jax.ShapeDtypeStruct(dims, BF16)
    ends = [shape(*raw[0].shape)] * 2
    sums = [shape(*((2, 2) if IS_SHARED[a] else (2,)), rows, columns[a]) for a in range(4)]
    full = [shape(width, columns[a]) for a in range(4)] * 2
    rest = (
        [shape(4, here, width)] * 2
        + [shape(8 * here, columns[DOWN])] * 2
        + [shape(8, here, width), shape(8 * here, columns[GU]), shape(8, here, width)]
    )
    blocks = [shape(kinds, rows, columns[a]) for a in range(4)] * 6
    far = ends + sums + [shape(*pack.shape[1:]) for pack in packs] + full + rest + blocks
    near = [jax.ShapeDtypeStruct((1, width), F32)] * 2
    inner = lambda *dims: pltpu.VMEM(dims, BF16)
    block = lambda *lead: pltpu.VMEM(lead + (here, width), BF16)
    wide = pltpu.VMEM((here, width), F32)
    wires = 2 * 8 * count + 8 * kinds + 6 * (12 + width // group) + 80
    scratch = [
        pltpu.SemaphoreType.DMA((wires,)),
        pltpu.SemaphoreType.DMA((wires,)),
        pltpu.SemaphoreType.DMA((8 * kinds + 60,)),
        inner(width, columns[DOWN]),
        inner(width, columns[OUT]),
        inner(width, columns[GU]),
        block(4),
        block(8),
        block(8),
        block(8),
        pltpu.VMEM((columns[QKV], tokens), F32),
        inner(8 * here, columns[GU]),
        inner(8 * here, columns[DOWN]),
    ]
    scratch += [inner(columns[QKV], tokens)] * 2 + [inner(tokens, head_width)] * 2
    scratch += [pltpu.VMEM((heads, tokens), F32)] * 2 + [wide] * 2
    scratch += [inner(head_width, length), inner(tokens, columns[QKV])]
    scratch += [inner(kinds, rows, columns[a]) for a in range(4)] + [inner(rows, max(columns))]
    scratch += [wide] * 3 + [block()] * 3
    sums_of = count.bit_length() + 1
    scratch += [
        pltpu.VMEM((2, 2, 1, width), F32),
        pltpu.VMEM((4, width), F32),
        pltpu.VMEM((sums_of + 1, 4, width), F32),
        pltpu.VMEM((sums_of, 4, width), F32),
    ]
    part = inner(here // 2, width)
    scratch += [block(), block(), block(4), block(3), block(), block(), part, part, block(), part]
    results = pl.pallas_call(
        functools.partial(layers_kernel, count, heads, group),
        out_shape=far + near,
        in_specs=[anywhere] * 8 + [inside] * 4,
        out_specs=[anywhere] * len(far) + [inside] * 2,
        scratch_shapes=scratch,
        compiler_params=pltpu.CompilerParams(
            collective_id=0, has_side_effects=True, vmem_limit_bytes=62 * 1024 * 1024
        ),
    )(*packs, *raw, *tables, owners[:, :, None], owners[:, None, :])
    return results[:2], results[2:6], results[-2:]


def unit_tiles(units, section, shared):
    tiles = units // 256
    first = section * units // 128 + shared * tiles
    return [(first + j) * 128 for j in range(tiles)], section * units + 256 * tiles + shared * 64


def pack_kernel(w_query, keyval, w_out, w_gate_up, w_down, qkv, out, gate_up, down):
    half = qkv.shape[2] - 2 * HEAD_SIZE
    units = w_down.shape[2] // 2
    for section in range(2):
        at = slice(section * half, (section + 1) * half)
        place = slice(section * HEAD_SIZE, (section + 1) * HEAD_SIZE)
        qkv[section, :, :half] = w_query[0, :, at]
        qkv[section, :, half:] = jnp.concatenate([keyval[0, :, 0, place], keyval[0, :, 1, place]], 1)
        out[section] = w_out[0, :, at]
        for shared in range(2):
            tiles, tail = unit_tiles(units, section, shared)
            for j, first in enumerate(tiles):
                for kind in range(2):
                    at = slice(256 * j + 128 * kind, 256 * j + 128 * kind + 128)
                    gate_up[section, shared, :, at] = w_gate_up[0, :, kind, first : first + 128]
                down[section, shared, :, 128 * j : 128 * j + 128] = w_down[0, :, first : first + 128]
            end = slice(tail, tail + 64)
            gate_up[section, shared, :, 256 * len(tiles) :] = jnp.concatenate(
                [w_gate_up[0, :, 0, end], w_gate_up[0, :, 1, end]], 1
            )
            some = w_down[0, :, end]
            down[section, shared, :, 128 * len(tiles) :] = jnp.concatenate(
                [some, jnp.zeros_like(some)], 1
            )


def unpack_kernel(qkv, out, gate_up, down, w_query, keyval, w_out, w_gate_up, w_down):
    half = qkv.shape[2] - 2 * HEAD_SIZE
    units = w_down.shape[2] // 2
    for section in range(2):
        at = slice(section * half, (section + 1) * half)
        w_query[0, :, at] = qkv[section, :, :half].astype(F32)
        w_out[0, :, at] = out[section].astype(F32)
        for shared in range(2):
            tiles, tail = unit_tiles(units, section, shared)
            for j, first in enumerate(tiles):
                for kind in range(2):
                    at = slice(256 * j + 128 * kind, 256 * j + 128 * kind + 128)
                    w_gate_up[0, :, kind, first : first + 128] = gate_up[section, shared, :, at].astype(F32)
                w_down[0, :, first : first + 128] = down[section, shared, :, 128 * j : 128 * j + 128].astype(F32)
        tiles, tail = unit_tiles(units, section, 0)
        last = slice(256 * len(tiles), 256 * len(tiles) + 128)
        both = [gate_up[section, shared, :, last].astype(F32) for shared in range(2)]
        w_gate_up[0, :, 0, tail : tail + 128] = jnp.concatenate([both[0][:, :64], both[1][:, :64]], 1)
        w_gate_up[0, :, 1, tail : tail + 128] = jnp.concatenate([both[0][:, 64:], both[1][:, 64:]], 1)
        at = slice(128 * len(tiles), 128 * len(tiles) + 64)
        w_down[0, :, tail : tail + 128] = jnp.concatenate(
            [down[section, shared, :, at].astype(F32) for shared in range(2)], 1
        )
    for kind in range(2):
        start = half + kind * HEAD_SIZE
        keyval[0, :, kind, :] = jnp.concatenate(
            [qkv[section, :, start : start + HEAD_SIZE].astype(F32) for section in range(2)], 1
        )


def row_specs(shapes, step):
    specs = []
    for dims, axis in shapes:
        block = tuple(step if i == axis else size for i, size in enumerate(dims))
        specs.append(
            pl.BlockSpec(block, functools.partial(lambda n, a, i: tuple(i if k == a else 0 for k in range(n)), len(dims), axis))
        )
    return specs


def packed(raw, kernel, outs, raw_first):
    rows = raw[0].shape[1] if raw_first else raw[0].shape[-2]
    step = min(rows, 64)
    wide = [(block.shape, 1) for block in (raw if raw_first else outs)]
    narrow = [(block.shape, len(block.shape) - 2) for block in (outs if raw_first else raw)]
    first, second = row_specs(wide, step), row_specs(narrow, step)
    return pl.pallas_call(
        kernel,
        grid=(rows // step,),
        out_shape=outs,
        in_specs=first if raw_first else second,
        out_specs=second if raw_first else first,
        compiler_params=pltpu.CompilerParams(vmem_limit_bytes=62 * 1024 * 1024),
    )(*raw)


def shards(
    layer_in,
    out_grad,
    doc_lengths,
    attn_gain,
    w_query,
    keyval_weight,
    w_out,
    mlp_gain,
    w_gate_up,
    w_down,
):
    micro, seqs, here, columns = layer_in.shape
    length = here * lax.axis_size("tensor")
    rows = w_query.shape[1]
    head_width = w_query.shape[2] // 2
    units = w_down.shape[2] // 4
    shape = jax.ShapeDtypeStruct
    raw = [w_query, keyval_weight, w_out, w_gate_up, w_down]
    packs = packed(
        raw,
        pack_kernel,
        [
            shape((2, rows, head_width + 2 * HEAD_SIZE), BF16),
            shape((2, rows, head_width), BF16),
            shape((2, 2, rows, 2 * units), BF16),
            shape((2, 2, rows, units + -units % 128), BF16),
        ],
        True,
    )
    owners = owners_of(doc_lengths.reshape(micro * seqs, -1), length)
    tables = rope_tables(length)
    (layer_out, in_grad), sums, (attn_term, mlp_term) = both_layers(
        packs, [layer_in, out_grad, attn_gain, mlp_gain], tables, owners
    )
    grads = packed(sums, unpack_kernel, [shape(block.shape, F32) for block in raw], False)
    grad_q, grad_kv, grad_o, grad_gu, grad_d = grads
    return layer_out, in_grad, attn_term, grad_q, grad_kv, grad_o, mlp_term, grad_gu, grad_d


def solution(mesh):
    activation = P(None, "dp", "tensor", "section")
    matrix = P("section", "dp", "tensor")
    stacked = P("section", "dp", None, "tensor")
    gain = P("section", None)
    return jax.shard_map(
        shards,
        mesh=mesh,
        in_specs=(
            activation,
            activation,
            P(None, "dp", None),
            gain,
            matrix,
            stacked,
            matrix,
            gain,
            stacked,
            matrix,
        ),
        out_specs=(
            activation,
            activation,
            gain,
            matrix,
            stacked,
            matrix,
            gain,
            stacked,
            matrix,
        ),
        check_vma=False,
    )
```

```python
import functools

import jax
import jax.numpy as jnp
from jax import lax
from jax.experimental import pallas as pl
from jax.experimental.pallas import tpu as pltpu
from jax.sharding import PartitionSpec as P

HEAD_SIZE = 64
NORM_EPSILON = 1e-05
ROPE_BASE = 10000.0
MASK_FILL = -1e30
FACTOR = HEAD_SIZE ** (-0.5)
BF16 = jnp.bfloat16
F32 = jnp.float32

def rope_tables(token_length):
    middle = HEAD_SIZE // 2
    frequency = ROPE_BASE ** (-(jnp.arange(middle, dtype=F32) * 2.0) / HEAD_SIZE)
    angles = frequency[:, None] * jnp.arange(token_length, dtype=F32)[None, :]
    return (
        jnp.concatenate([jnp.cos(angles), jnp.cos(angles)], 0),
        jnp.concatenate([jnp.sin(angles), jnp.sin(angles)], 0),
    )


def owners_of(lengths, token_length):
    bounds = jnp.cumsum(lengths, -1)
    places = jnp.arange(token_length, dtype=jnp.int32)
    return jnp.sum((places[None, :, None] >= bounds[:, None, :]).astype(jnp.int32), -1)


def visible_block(owner_col, owner_row):
    length = owner_col.shape[0]
    key_place = lax.broadcasted_iota(jnp.int32, (length, length), 0)
    query_place = lax.broadcasted_iota(jnp.int32, (length, length), 1)
    return (owner_col == owner_row) & (key_place <= query_place)


def rope(u, cosine, sine):
    half = HEAD_SIZE // 2
    return u * cosine + jnp.concatenate([-u[half:], u[:half]], 0) * sine


def rope_back(u, cosine, sine):
    half = HEAD_SIZE // 2
    w = u * sine
    return u * cosine + jnp.concatenate([w[half:], -w[:half]], 0)


def normed(values, gain):
    inverse = lax.rsqrt(jnp.mean(values * values, -1, keepdims=True) + NORM_EPSILON)
    return (values * inverse * gain).astype(BF16)


def norm_back(grad, values, gain):
    inverse = lax.rsqrt(jnp.mean(values * values, -1, keepdims=True) + NORM_EPSILON)
    scaled = values * inverse
    gained = grad * gain
    into = inverse * (gained - scaled * jnp.mean(gained * scaled, -1, keepdims=True))
    return into, jnp.sum(grad * scaled, 0, keepdims=True)


def crossed(values, group):
    count = values.shape[-1] // group
    return jnp.concatenate(
        [values[:, (g ^ 1) * group : ((g ^ 1) + 1) * group] for g in range(count)], 1
    )


def reordered(values, count):
    me = lax.axis_index("dp")
    group = values.shape[-1] // count
    while group < values.shape[-1]:
        values = jnp.where(lax.rem(me, 2) == 1, crossed(values, group), values)
        me, group = me // 2, group * 2
    return values


def dot_t(left, right):
    return lax.dot_general(left, right, (((1,), (1,)), ((), ())), preferred_element_type=F32)


def dot_n(left, right):
    return jnp.dot(left, right, preferred_element_type=F32)


def dot_tn(left, right):
    return lax.dot_general(left, right, (((0,), (0,)), ((), ())), preferred_element_type=F32)


class Hops:
    def __init__(self, send, recv):
        self.send, self.recv, self.count, self.started = send, recv, 0, []
        self.index = {name: lax.axis_index(name) for name in ("section", "dp", "tensor")}
        self.other = 1 - self.index["section"]

    def to(self, offset):
        dp = self.index["dp"]
        for bit in range(offset.bit_length()):
            if offset >> bit & 1:
                low = lax.rem(dp // (1 << bit), 2)
                dp = dp + (1 - 2 * low) * (1 << bit)
        return (self.index["section"], dp, self.index["tensor"])

    def across(self):
        return (self.other, self.index["dp"], self.index["tensor"])

    def core(self):
        return (self.index["section"], self.index["dp"], 1 - self.index["tensor"])

    def at(self, source, target, device, index):
        return pltpu.make_async_remote_copy(
            src_ref=source,
            dst_ref=target,
            send_sem=self.send.at[index],
            recv_sem=self.recv.at[index],
            device_id=device,
            device_id_type=pl.DeviceIdType.MESH,
        )

    def claim(self, number=1):
        self.count += number
        return self.count - number

    def start(self, source, target, device):
        copy = self.at(source, target, device, self.claim())
        copy.start()
        self.started.append(copy)
        return copy

    def start_either(self, choice, first, second, target, device):
        index = self.claim()
        copy = self.at(first, target, device, index)
        backup = self.at(second, target, device, index)
        pl.when(choice)(copy.start)
        pl.when(jnp.logical_not(choice))(backup.start)
        self.started.append(copy)
        return copy

    def sent(self, copies):
        copies = list(copies)
        for copy in copies:
            copy.wait_send()
        gone = {id(copy) for copy in copies}
        self.started = [copy for copy in self.started if id(copy) not in gone]

    def greet(self, offsets):
        barrier = pltpu.get_barrier_semaphore()
        devices = [self.to(offset) for offset in offsets] + [self.across(), self.core()]
        for device in devices:
            pl.semaphore_signal(
                barrier, inc=1, device_id=device, device_id_type=pl.DeviceIdType.MESH
            )
        pl.semaphore_wait(barrier, len(devices))

    def drain(self):
        for copy in self.started:
            copy.wait_send()


class Local:
    AT_ONCE = 6

    def __init__(self, sems):
        self.sems, self.count = sems, self.AT_ONCE

    def claim(self, number=1):
        self.count += number
        return self.count - number

    def make(self, source, target):
        return pltpu.make_async_copy(source, target, self.sems.at[self.claim()])

    def start(self, source, target):
        copy = self.make(source, target)
        copy.start()
        return copy

    def now(self, *moves):
        waits = []
        for index, move in enumerate(moves):
            make = lambda source: pltpu.make_async_copy(source, move[-1], self.sems.at[index])
            copy = make(move[-2])
            if len(move) == 2:
                copy.start()
            else:
                pl.when(move[0])(make(move[1]).start)
                pl.when(jnp.logical_not(move[0]))(copy.start)
            waits.append(copy)
        for copy in waits:
            copy.wait()


def reached(count):
    return [1] + [2 * k for k in range(1, count // 2)]


class Spread:
    def __init__(self, hops, local, own, turned, group):
        self.hops, self.local, self.own, self.turned, self.group = hops, local, own, turned, group

    def four(self, rows, slots):
        hops, own = self.hops, self.own
        section, tensor = hops.index["section"], hops.index["tensor"]
        own[...] = rows
        slot = 2 * section + tensor
        self.over_y = hops.start(own, slots.at[slot], hops.across())
        self.over_core = hops.start(own, slots.at[slot], hops.core())
        self.keep = self.local.start(own, slots.at[slot])

    def four_end(self, slots):
        hops = self.hops
        self.over_y.wait_recv()
        across = 2 * (1 - hops.index["section"]) + hops.index["tensor"]
        last = hops.start(slots.at[across], slots.at[across], hops.core())
        self.over_core.wait_recv()
        last.wait_recv()
        self.keep.wait()
        hops.sent([self.over_y, self.over_core, last])

    def halves(self):
        half = self.own.shape[0] // 2
        return pl.ds(0, half), pl.ds(half, half)

    def eight(self, rows, slots):
        hops, own, turned = self.hops, self.own, self.turned
        own[...] = rows
        turned[...] = crossed(rows, self.group)
        lo, hi = self.halves()
        y, z, core = hops.across(), hops.to(2), hops.core()
        self.over = [
            hops.start(own.at[hi], slots.at[2, hi], y),
            hops.start(turned.at[lo], slots.at[4, lo], z),
            hops.start(own.at[lo], slots.at[2, lo], y),
            hops.start(turned.at[hi], slots.at[4, hi], z),
        ]
        self.cores = [hops.start(own, slots.at[1], core)]
        self.keep = self.local.start(own, slots.at[0])

    def eight_middle(self, slots):
        hops, group = self.hops, self.group
        lo, hi = self.halves()
        self.over[0].wait_recv()
        self.diag = [
            hops.start(
                slots.at[2, hi, pl.ds(g * group, group)],
                slots.at[6, hi, pl.ds((g ^ 1) * group, group)],
                hops.to(2),
            )
            for g in range(self.own.shape[1] // group)
        ]
        self.over[1].wait_recv()
        self.diag.append(hops.start(slots.at[4, lo], slots.at[6, lo], hops.across()))

    def eight_end(self, slots):
        hops = self.hops
        core = hops.core()
        self.over[2].wait_recv()
        self.cores.append(hops.start(slots.at[2], slots.at[3], core))
        self.over[3].wait_recv()
        self.cores.append(hops.start(slots.at[4], slots.at[5], core))
        for copy in self.diag:
            copy.wait_recv()
        self.cores.append(hops.start(slots.at[6], slots.at[7], core))
        for copy in self.cores:
            copy.wait_recv()
        self.keep.wait()
        hops.sent(self.over + self.diag + self.cores)


class Sums:
    def __init__(self, hops, partial, core, out, from_y, from_z, part_y, part_z, group):
        self.hops, self.partial, self.core, self.out, self.group = hops, partial, core, out, group
        self.from_y, self.from_z, self.part_y, self.part_z = from_y, from_z, part_y, part_z

    def four(self):
        hops, core, out, from_y, partial = self.hops, self.core, self.out, self.from_y, self.partial
        section, tensor = hops.index["section"], hops.index["tensor"]
        slots = [2 * section, 2 * (1 - section)]
        far = {
            c: hops.start(partial.at[slots[c] + 1 - tensor], core.at[c], hops.core()) for c in (1, 0)
        }
        far[1].wait_recv()
        out[0] = (partial[slots[1] + tensor].astype(F32) + core[1].astype(F32)).astype(BF16)
        over_y = hops.start(out.at[0], from_y, hops.across())
        far[0].wait_recv()
        over_y.wait_recv()
        total = (
            partial[slots[0] + tensor].astype(F32) + core[0].astype(F32) + from_y[...].astype(F32)
        )
        hops.sent([far[0], far[1], over_y])
        return total

    def halves(self):
        half = self.out.shape[1] // 2
        return pl.ds(0, half), pl.ds(half, half)

    def added(self, c, rows):
        return self.partial[2 * c, rows, :].astype(F32) + self.core[c, rows, :].astype(F32)

    def eight(self):
        hops, out, group = self.hops, self.out, self.group
        lo, hi = self.halves()
        y, z = hops.across(), hops.to(2)
        self.far = {
            c: hops.start(self.partial.at[2 * c + 1], self.core.at[c], hops.core())
            for c in (3, 1, 2, 0)
        }
        self.far[3].wait_recv()
        out[2, lo, :] = self.added(3, lo).astype(BF16)
        self.diag_y = hops.start(out.at[2, lo], self.part_y, y)
        out[2, hi, :] = crossed(self.added(3, hi), group).astype(BF16)
        self.diag_z = hops.start(out.at[2, hi], self.part_z, z)
        self.far[1].wait_recv()
        out[0, lo, :] = self.added(1, lo).astype(BF16)
        self.over = [hops.start(out.at[0, lo], self.from_y.at[lo], y)]
        self.far[2].wait_recv()
        out[1, hi, :] = crossed(self.added(2, hi), group).astype(BF16)
        self.over.append(hops.start(out.at[1, hi], self.from_z.at[hi], z))

    def eight_middle(self):
        hops, out, group = self.hops, self.out, self.group
        lo, hi = self.halves()
        self.diag_y.wait_recv()
        out[1, lo, :] = crossed(self.added(2, lo) + self.part_y[...].astype(F32), group).astype(BF16)
        self.over.append(hops.start(out.at[1, lo], self.from_z.at[lo], hops.to(2)))
        self.diag_z.wait_recv()
        out[0, hi, :] = (self.added(1, hi) + self.part_z[...].astype(F32)).astype(BF16)
        self.over.append(hops.start(out.at[0, hi], self.from_y.at[hi], hops.across()))

    def eight_end(self):
        self.far[0].wait_recv()
        for copy in self.over:
            copy.wait_recv()
        total = (
            self.partial[0].astype(F32)
            + self.core[0].astype(F32)
            + self.from_y[...].astype(F32)
            + self.from_z[...].astype(F32)
        )
        self.hops.sent(list(self.far.values()) + [self.diag_y, self.diag_z] + self.over)
        return total


QKV, OUT, GU, DOWN = range(4)
IS_SHARED = (False, False, True, True)


def others(k, kinds):
    return [k] + (list(range(4, kinds)) if k == 1 else [])


class Gather:
    def __init__(self, hops, local, count, packs, crossed_over, full):
        self.hops, self.local, self.packs, self.over, self.full = hops, local, packs, crossed_over, full
        self.kinds = count // 2
        self.arrived, self.have = {}, set()
        self.half = lax.rem(hops.index["dp"] // 2, 2)
        self.rows = packs[0].shape[-2]

    def cross(self, a):
        hops = self.hops
        self.arrived[a] = hops.start(self.packs[a].at[hops.other], self.over[a], hops.across())

    def block(self, a, layer, r):
        return self.full[layer][a].at[pl.ds(r * self.rows, self.rows)]

    def source(self, a, other):
        if a not in self.have:
            self.have.add(a)
            self.arrived[a].wait_recv()
        section = self.hops.index["section"]
        if not IS_SHARED[a]:
            return self.packs[a].at[section], self.over[a]
        which = 1 - self.half if other else self.half
        return self.packs[a].at[section, which], self.over[a].at[which]

    def straight(self, a, layer):
        first, second = self.source(a, False)
        here = self.hops.index["section"] == layer
        self.arrived[a, layer, "x", 0] = self.hops.start_either(
            here, first, second, self.block(a, layer, 1), self.hops.to(1)
        )

    def begin(self, a, layer, step):
        for k in others(step, self.kinds):
            if IS_SHARED[a] or k == 1 or k % 2 == 0:
                first, second = self.source(a, k % 2 == 1)
                self.arrived[a, layer, k] = self.hops.start_either(
                    self.hops.index["section"] == layer,
                    first,
                    second,
                    self.block(a, layer, 2 * k),
                    self.hops.to(2 * k),
                )

    def onward(self, a, layer, step):
        hops = self.hops
        for k in others(step, self.kinds):
            self.arrived[a, layer, k].wait_recv()
            self.arrived[a, layer, "x", k] = hops.start(
                self.block(a, layer, 2 * k), self.block(a, layer, 2 * k + 1), hops.to(1)
            )
            if not IS_SHARED[a] and k % 2 == 0:
                self.arrived[a, layer, k + 1] = hops.start(
                    self.block(a, layer, 2 * k), self.block(a, layer, 2 * k + 2), hops.to(2)
                )

    def complete(self, a, layer):
        for k in range(self.kinds):
            self.arrived[a, layer, "x", k].wait_recv()

    def parts(self, a, layer, target):
        first, second = self.source(a, False)
        rest = pl.ds(self.rows, target.shape[0] - self.rows)
        here = self.hops.index["section"] == layer
        return [
            (here, first, second, target.at[pl.ds(0, self.rows)]),
            (self.full[layer][a].at[rest], target.at[rest]),
        ]


def attention_step(heads, qkv, place, cos, sin, visible, rotated, log_total):
    width = heads * HEAD_SIZE
    keys = rope(qkv[width : width + HEAD_SIZE, place], cos, sin).astype(BF16)
    values = qkv[width + HEAD_SIZE :, place].astype(BF16)
    rotated[width : width + HEAD_SIZE, place] = keys
    rotated[width + HEAD_SIZE :, place] = values
    attended = []
    for h in range(heads):
        at = slice(h * HEAD_SIZE, (h + 1) * HEAD_SIZE)
        queries = rope(qkv[at, place], cos, sin).astype(BF16)
        rotated[at, place] = queries
        score = dot_tn(keys, queries)
        score = jnp.where(visible, score * FACTOR, MASK_FILL)
        top = jnp.max(score, 0, keepdims=True)
        exponent = jnp.exp(score - top)
        total = jnp.sum(exponent, 0, keepdims=True)
        prob = (exponent * (1.0 / total)).astype(BF16)
        attended.append(dot_n(values, prob))
        log_total[h : h + 1, place] = top + jnp.log(total)
    return jnp.concatenate(attended, 0).T.astype(BF16)


def attention_back_step(heads, rotated, grad_att, place, cos, sin, visible, log_total):
    width = heads * HEAD_SIZE
    keys = rotated[width : width + HEAD_SIZE, place]
    values = rotated[width + HEAD_SIZE :, place]
    length = keys.shape[1]
    grad_keys = jnp.zeros((HEAD_SIZE, length), F32)
    grad_values = jnp.zeros((HEAD_SIZE, length), F32)
    found = []
    for h in range(heads):
        at = slice(h * HEAD_SIZE, (h + 1) * HEAD_SIZE)
        queries = rotated[at, place]
        grad = grad_att[at, :]
        score = jnp.where(visible, dot_tn(keys, queries) * FACTOR, MASK_FILL)
        prob = jnp.exp(score - log_total[h : h + 1, place])
        grad_prob = dot_tn(values, grad)
        inner = jnp.sum(prob * grad_prob, 0, keepdims=True)
        grad_score = (FACTOR * prob * (grad_prob - inner)).astype(BF16)
        found.append(rope_back(dot_n(keys, grad_score), cos, sin))
        grad_keys += dot_t(queries, grad_score)
        grad_values += dot_t(grad, prob.astype(BF16))
    found += [rope_back(grad_keys, cos, sin), grad_values]
    return jnp.concatenate(found, 0).T.astype(BF16)


def steps_of(names):
    found = []
    for name in names:
        letters = name.rstrip("0123456789")
        found.append((letters, *(int(digit) for digit in name[len(letters) :])))
    return found


ORDER = (
    "c0", "B002", "B001", "c1", "B012", "X01", "B102", "c2", "n0", "X00", "O001", "B101",
    "O002", "X20", "B202", "O003", "B201", "m0", "X11", "B111", "c3", "O202", "O102", "B301",
    "B011", "B303", "B203", "B312", "a0", "O101", "O103", "X10", "O201", "B112", "e0", "q0",
    "O303", "O011", "r0", "O301", "X30", "g0", "n1", "h0", "O203", "B302", "m1", "O012",
    "i0", "O112", "O302", "B212", "u0", "d0", "O113", "s0", "O111", "t0", "B211", "B311",
    "B213", "O013", "O212", "v0", "B313", "a1", "X31", "e1", "O211", "X21", "q1", "r1",
    "O213", "g1", "h1", "O311", "i1", "O313", "g2", "O312", "u1", "h2", "i2", "bl1",
    "S31", "bk1", "bp1", "E31", "bs1", "S21", "bt1", "E21", "Z311", "bv1", "ba1", "Z313",
    "be1", "bq1", "Z211", "Z312", "br1", "S11", "bg1", "bh1", "Z210", "Z213", "E11", "Z212",
    "E01", "Z310", "Y31", "S01", "bi1", "bl0", "bk0", "S30", "E30", "bp0", "bs0", "Z113",
    "Y21", "Z302", "Z013", "bt0", "Z111", "S20", "Z110", "Z011", "E20", "Z200", "Z303", "Z012",
    "bv0", "ba0", "Z112", "be0", "Z010", "Z201", "Z301", "Y01", "Z203", "Y11", "bq0", "Z202",
    "Z300", "E00", "S00", "E10", "br0", "bn0", "Y30", "bn1", "S10", "d1", "Z003", "bn2",
    "s1", "Z000", "Y20", "Z002", "Z103", "Z001", "Z101", "Z102", "Z100", "t1", "Y00", "Y10",
    "bn3", "w1", "bn4", "v1", "bn5", "w0",
)


def into_partial(block, w, partial, here, width, tile):
    @pl.loop(0, width // tile)
    def _(n):
        cut = pl.ds(pl.multiple_of(n * tile, tile), tile)
        some = dot_t(block[...], w[cut, :])
        partial[:, :, cut] = some.astype(BF16).reshape(partial.shape[0], here, tile)


def add_rows(target, left, right):
    rows = target.shape[0]
    step = min(32, rows)

    @pl.loop(0, rows // step)
    def _(i):
        at = pl.ds(pl.multiple_of(i * step, step), step)
        target[at, :] = (left[at, :].astype(F32) + right[at, :].astype(F32)).astype(BF16)


class Scatter:
    def __init__(self, hops, local, kept, staged, landed, distant, sums_out, one_block, term, rows):
        self.hops, self.local, self.kept, self.staged = hops, local, kept, staged
        self.landed, self.distant, self.sums_out = landed, distant, sums_out
        self.one_block, self.term, self.rows = one_block, term, rows
        self.kinds = kept[0].shape[0]
        self.half = lax.rem(hops.index["dp"] // 2, 2)
        self.section = hops.index["section"]
        self.copies, self.ending = {}, []

    def renew(self, a):
        assert (a, 1) in [entry[:2] for entry in self.ending]
        out = [self.copies[a, 1, "z", k] for k in range(1, self.kinds)]
        self.hops.sent([copy for copy in out if copy is not None])
        for b, layer, keep, away in self.ending:
            if (b, layer) == (a, 1):
                pl.when(self.section == layer)(keep.wait)
                pl.when(self.section != layer)(away.wait_send)

    def stage(self, a, layer):
        hops, local, rows, kept = self.hops, self.local, self.rows, self.kept
        if layer == 0 and rows % 128:
            self.renew(a)
        base, at = hops.claim(self.kinds), local.claim(self.kinds)
        cols = pl.ds(0, kept[a].shape[-1])
        source, target = self.staged[layer][a], self.landed[layer][a]

        @pl.loop(0, self.kinds)
        def _(k):
            if rows % 128:
                both = self.term(a, 2 * k, 2 * rows)
                self.one_block[:, cols] = both[rows:]
                kept[a][k] = both[:rows]
            else:
                self.one_block[:, cols] = self.term(a, 2 * k + 1, rows)
            keep = pltpu.make_async_copy(
                self.one_block.at[:, cols], source.at[k], local.sems.at[at + k]
            )
            keep.start()
            keep.wait()
            hops.at(source.at[k], target.at[k], hops.to(1), base + k).start()

        for k in range(self.kinds):
            copy = hops.at(source.at[k], target.at[k], hops.to(1), base + k)
            self.copies[a, layer, "x", k] = copy
            hops.started.append(copy)

    def evens(self, a, layer):
        if self.rows % 128:
            return
        if layer == 0:
            self.renew(a)

        @pl.loop(0, self.kinds)
        def _(k):
            self.kept[a][k] = self.term(a, 2 * k, self.rows)

    def fetch(self, a, source):
        block = self.one_block.at[:, pl.ds(0, self.kept[a].shape[-1])]
        self.local.now((source, block))
        return block

    def meet(self, a, layer, step):
        hops, kept, copies = self.hops, self.kept[a], self.copies
        far = self.distant[layer][a]
        steps = [0] if step == 0 else list(reversed(others(step, self.kinds)))
        for k in steps:
            copies[a, layer, "x", k].wait_recv()
            add_rows(kept.at[k], kept.at[k], self.fetch(a, self.landed[layer][a].at[k]))
            if not IS_SHARED[a] and k % 2 == 0 and k:
                copies[a, layer, "z", k + 1].wait_recv()
                add_rows(kept.at[k], kept.at[k], self.fetch(a, far.at[k + 1]))
            if k:
                passed = not IS_SHARED[a] and k % 2 == 1 and k > 1
                copies[a, layer, "z", k] = hops.start(
                    kept.at[k], far.at[k], hops.to(2 if passed else 2 * k)
                )

    def deliver(self, a, layer):
        hops, kept, copies = self.hops, self.kept[a], self.copies
        far = self.distant[layer][a]
        mine, other = [], []
        for k in range(1, self.kinds):
            if IS_SHARED[a] or k == 1 or k % 2 == 0:
                copies[a, layer, "z", k].wait_recv()
                (other if IS_SHARED[a] and k % 2 else mine).append(k)
        for k in mine:
            add_rows(kept.at[0], kept.at[0], self.fetch(a, far.at[k]))
        pieces = [kept.at[0]]
        if IS_SHARED[a]:
            hops.sent([copies[a, layer, "z", 1]])
            copies[a, layer, "z", 1] = None
            self.local.now((far.at[other[0]], kept.at[1]))
            for k in other[1:]:
                add_rows(kept.at[1], kept.at[1], self.fetch(a, far.at[k]))
            pieces.append(kept.at[1])
        for number, piece in enumerate(pieces):
            which = self.half if number == 0 else 1 - self.half
            target = self.sums_out[a].at[self.section]
            if IS_SHARED[a]:
                target = self.sums_out[a].at[self.section, which]
            keep = self.local.make(piece, target)
            away = hops.at(piece, target, hops.across(), hops.claim())
            pl.when(self.section == layer)(keep.start)
            pl.when(self.section != layer)(away.start)
            self.ending.append((a, layer, keep, away))

    def end(self):
        for a, layer, keep, away in self.ending:
            pl.when(self.section == layer)(away.wait_recv)
            if layer == 0:
                pl.when(self.section == layer)(keep.wait)
                pl.when(self.section != layer)(away.wait_send)


def layers_kernel(count, heads, group, *refs):
    refs = list(refs)
    take = lambda number: [refs.pop(0) for _ in range(number)]
    packs, raw_rows, raw_gains = take(4), take(2), take(2)
    cosine, sine, owner_col, owner_row = take(4)
    ends, sums_out = take(2), take(4)
    crossed_over, full = take(4), (take(4), take(4))
    rows_attn_out, hidden_out, (rows_mlp_out, gate_up_out, grad_out) = take(2), take(2), take(3)
    staged, landed, distant = [(take(4), take(4)) for _ in range(3)]
    gain_sums = take(2)
    send, recv, sems = take(3)
    w_low, w_out, w_gu = take(3)
    slots4, slots8, partial, rows_mlp = take(4)
    qkv, gate_up, hidden = take(3)
    rotated, attended, log_total, middles = [take(2) for _ in range(4)]
    grad_att, grad_qkv = take(2)
    kept, (one_block,) = take(4), take(1)
    entering, handed, grad_middle = take(3)
    raw_whole, cotangent, through = take(3)
    gain_whole, gains, gain_terms, gain_landed = take(4)
    own, turned, core, out, from_y, from_z, part_y, part_z, last_z, last_part = take(10)
    hops, local = Hops(send, recv), Local(sems)
    hops.greet(reached(count))
    spread = Spread(hops, local, own, turned, group)
    sums = Sums(hops, partial, core, out, from_y, from_z, part_y, part_z, group)
    sums_last = Sums(hops, partial, core, out, from_y, last_z, part_y, last_part, group)
    gather = Gather(hops, local, count, packs, crossed_over, full)
    section = hops.index["section"]
    here, width = own.shape
    rows = width // count
    length = cosine.shape[1]
    seqs = slots4.shape[0] * here // length
    per_seq = length // here
    tile = 512
    units = hidden.shape[1]
    real = gate_up.shape[1] // 2
    whole = real // 128
    rest = real - whole * 128
    split = rotated[0].shape[0]
    rows_attn = partial.at[pl.ds(4, 4)]
    stores = []

    def store(source, target):
        stores.append(local.start(source, target))

    def settle():
        for copy in stores:
            copy.wait()
        stores.clear()

    def span(i, size):
        return pl.ds(pl.multiple_of(i * size, size), size)

    w_qkv = w_low.at[:, pl.ds(0, split)]

    def project(layer):
        gather.complete(QKV, layer)
        gather.complete(OUT, layer)
        local.now(*gather.parts(QKV, layer, w_qkv), *gather.parts(OUT, layer, w_out))

        @pl.loop(0, seqs)
        def _(i):
            block = slots4[pl.ds(i * per_seq, per_seq)].reshape(length, width)
            place = span(i, length)
            qkv[:, place] = dot_n(block, w_low[:, :split]).T
            visible = visible_block(owner_col[i], owner_row[i])
            attended[layer][place, :] = attention_step(
                heads, qkv, place, cosine[...], sine[...], visible, rotated[layer], log_total[layer]
            )

        store(slots4, rows_attn_out[layer])

        @pl.loop(0, width // tile)
        def _(n):
            cut = span(n, tile)
            for i in range(seqs):
                some = dot_t(attended[layer][i * length : (i + 1) * length, :], w_out[cut, :])
                partial[i * per_seq : (i + 1) * per_seq, :, cut] = some.astype(BF16).reshape(
                    per_seq, here, tile
                )

    def expand(layer):
        gather.complete(GU, layer)
        local.now(*gather.parts(GU, layer, w_gu))

        block = slots8[...].reshape(slots8.shape[0] * here, width)

        @pl.loop(0, whole)
        def _(n):
            cut = span(n, 256)
            both = dot_n(block, w_gu[:, cut])
            gate_up[:, cut] = both.astype(BF16)
            gate, up = both[:, :128], both[:, 128:]
            hidden[:, span(n, 128)] = (gate * jax.nn.sigmoid(gate) * up).astype(BF16)

        if rest:
            both = dot_n(block, w_gu[:, whole * 256 :])
            gate_up[:, whole * 256 :] = both.astype(BF16)
            gate, up = both[:, :rest], both[:, rest:]
            some = (gate * jax.nn.sigmoid(gate) * up).astype(BF16)
            hidden[:, whole * 128 :] = jnp.concatenate([some, jnp.zeros_like(some)], 1)

        if layer == 0:
            store(slots8, rows_mlp_out)
            store(gate_up, gate_up_out)
        else:
            rows_mlp[...] = slots8[...]
        store(hidden, hidden_out[layer])

    def entry(layer):
        return entering if layer == 0 else handed

    waiting = {}

    def bring(number):
        target = raw_whole.at[:, span(section, width // 2)]
        waiting[number] = [
            hops.start(raw_rows[number].at[hops.other, 0], target, hops.across()),
            local.start(raw_rows[number].at[section, 0], target),
        ]
        if number == 0:
            for kind in range(2):
                waiting[number] += [
                    hops.start(raw_gains[kind], gain_whole.at[section, kind], hops.across()),
                    local.start(raw_gains[kind], gain_whole.at[section, kind]),
                ]

    def brought(number):
        for place, copy in enumerate(waiting[number]):
            copy.wait() if place % 2 else copy.wait_recv()
        rows_here = reordered(raw_whole[...].astype(F32), count)
        if number == 0:
            entering[...] = rows_here
            for layer in range(2):
                for kind in range(2):
                    mark = 2 * layer + kind
                    gains[mark : mark + 1, :] = reordered(gain_whole[layer, kind], count)
        else:
            cotangent[...] = rows_here.astype(BF16)

    def gain(layer, kind):
        mark = 2 * layer + kind
        return gains[mark : mark + 1, :]

    def ready(layer):
        settle()
        if layer == 1:
            local.now((grad_out, slots8))
        else:
            local.now((gate_up_out, gate_up), (hidden_out[0], hidden), (rows_mlp_out, rows_mlp))

    def widen(layer):
        if layer == 1:
            gather.complete(DOWN, 1)
        local.now(*gather.parts(DOWN, layer, w_low))

        @pl.loop(0, slots8.shape[0] // 2)
        def _(c):
            block = slots8[pl.ds(c * 2, 2)].reshape(2 * here, width)
            place = span(c, 2 * here)
            grad_hidden = dot_n(block, w_low[...]).astype(BF16).astype(F32)

            def back(grad, gate, up):
                gate, up = gate.astype(F32), up.astype(F32)
                sig = jax.nn.sigmoid(gate)
                return [
                    (grad * up * sig * (1.0 + gate * (1.0 - sig))).astype(BF16),
                    (grad * (gate * sig)).astype(BF16),
                ]

            for n in range(whole):
                at = slice(n * 256, n * 256 + 256)
                both = gate_up[place, at]
                gate_up[place, at] = jnp.concatenate(
                    back(grad_hidden[:, n * 128 : n * 128 + 128], both[:, :128], both[:, 128:]), 1
                )
            if rest:
                both = gate_up[place, whole * 256 :]
                gate_up[place, whole * 256 :] = jnp.concatenate(
                    back(grad_hidden[:, whole * 128 : real], both[:, :rest], both[:, rest:]), 1
                )

    def attend(layer):
        local.now(
            *gather.parts(OUT, layer, w_out),
            *gather.parts(QKV, layer, w_qkv),
            (rows_attn_out[layer], rows_attn),
        )

        @pl.loop(0, seqs)
        def _(i):
            block = slots4[pl.ds(i * per_seq, per_seq)].reshape(length, width)
            place = span(i, length)
            grad_att[...] = dot_n(block, w_out[...]).T.astype(BF16)
            visible = visible_block(owner_col[i], owner_row[i])
            grad_qkv[place, :] = attention_back_step(
                heads, rotated[layer], grad_att, place, cosine[...], sine[...], visible, log_total[layer]
            )

        @pl.loop(0, width // tile)
        def _(n):
            cut = span(n, tile)
            for i in range(seqs):
                some = dot_t(grad_qkv[i * length : (i + 1) * length, :], w_low[cut, :split])
                partial[i * per_seq : (i + 1) * per_seq, :, cut] = some.astype(BF16).reshape(
                    per_seq, here, tile
                )

    working = [1]

    def term(a, r, size):
        slots, right = {
            QKV: (rows_attn, grad_qkv),
            OUT: (slots4, attended[working[0]]),
            GU: (rows_mlp, gate_up),
            DOWN: (slots8, hidden),
        }[a]
        cut = pl.ds(pl.multiple_of(r * rows, max(rows, 128)), size)
        return dot_tn(slots[:, :, cut].reshape(slots.shape[0] * here, size), right[...]).astype(BF16)

    scatter = Scatter(
        hops, local, kept, staged, landed, distant, sums_out, one_block, term, rows
    )

    def back_through(total, source, values, layer, kind, result):
        into, term_row = norm_back(total, values, gain(layer, kind))
        mark = 2 * layer + kind
        gain_terms[0, mark : mark + 1, :] = term_row
        result[...] = (source + into).astype(result.dtype)

    leaving = []

    def leave(number, block):
        block[...] = reordered(block[...].astype(F32), count).astype(BF16)
        target = ends[number].at[section, 0]
        leaving.append(local.start(block.at[:, span(section, width // 2)], target))
        leaving.append(hops.start(block.at[:, span(hops.other, width // 2)], target, hops.across()))

    gain_places, offset = [hops.core(), hops.across()], 1
    while offset < count:
        gain_places.append(hops.to(offset))
        offset *= 2
    gain_moves = []

    def add_gains(step):
        for number in range(step, len(gain_places) + 1) if step == 5 else [step]:
            if number == 0:
                gain_terms[0] = reordered(gain_terms[0], count)
            else:
                gain_moves[-1].wait_recv()
                gain_terms[number] = gain_terms[number - 1] + gain_landed[number - 1]
            if number < len(gain_places):
                gain_moves.append(
                    hops.start(gain_terms.at[number], gain_landed.at[number], gain_places[number])
                )
        if step == 5:
            total = gain_terms[len(gain_places)]
            mine = jnp.where(section == 0, total[0:2], total[2:4])
            for kind in range(2):
                gain_sums[kind][...] = mine[kind : kind + 1]

    for name, *at in steps_of(ORDER):
        layer = at[0]
        if name == "c":
            gather.cross(*at)
        elif name == "X":
            gather.straight(*at)
        elif name == "B":
            gather.begin(*at)
        elif name == "O":
            gather.onward(*at)
        elif name == "n":
            bring(*at)
        elif name == "m":
            brought(*at)
        elif name == "a":
            spread.four(normed(entry(layer)[...], gain(layer, 0)), slots4)
        elif name in ("e", "be"):
            spread.four_end(slots4)
        elif name == "q":
            project(layer)
        elif name == "r":
            middles[layer][...] = entry(layer)[...] + sums.four()
        elif name == "g":
            if layer == 2:
                spread.eight(cotangent[...], grad_out)
            else:
                spread.eight(normed(middles[layer][...], gain(layer, 1)), slots8)
        elif name == "h":
            spread.eight_middle(grad_out if layer == 2 else slots8)
        elif name == "i":
            spread.eight_end(grad_out if layer == 2 else slots8)
        elif name == "u":
            expand(layer)
        elif name == "d":
            if layer == 0:
                gather.complete(DOWN, 0)
            else:
                local.now((hidden_out[1], hidden))
            local.now(*gather.parts(DOWN, layer, w_low))
            into_partial(hidden, w_low, partial, here, width, tile // 2)
        elif name == "s":
            settle()
            (sums_last if layer == 1 else sums).eight()
        elif name == "t":
            (sums_last if layer == 1 else sums).eight_middle()
        elif name == "v":
            if layer == 1:
                raw_whole[...] = (middles[1][...] + sums_last.eight_end()).astype(BF16)
            else:
                handed[...] = (middles[0][...] + sums.eight_end()).astype(BF16).astype(F32)
        elif name == "bl":
            working[0] = layer
            ready(layer)
        elif name == "bk":
            widen(layer)
        elif name == "S":
            scatter.stage(*at)
        elif name == "E":
            scatter.evens(*at)
        elif name == "Z":
            scatter.meet(*at)
        elif name == "Y":
            scatter.deliver(*at)
        elif name == "bp":
            if layer == 0:
                local.now(*gather.parts(GU, 0, w_gu))
            into_partial(gate_up, w_gu, partial, here, width, tile // 2)
        elif name == "bs":
            sums.eight()
        elif name == "bt":
            sums.eight_middle()
        elif name == "bv":
            total = sums.eight_end()
            source = (cotangent if layer == 1 else through)[...].astype(F32)
            back_through(total, source, middles[layer][...], layer, 1, grad_middle)
        elif name == "ba":
            spread.four(grad_middle[...].astype(BF16), slots4)
        elif name == "bq":
            attend(layer)
        elif name == "br":
            back_through(sums.four(), grad_middle[...], entry(layer)[...], layer, 0, through)
        elif name == "bg":
            spread.eight(through[...], slots8)
        elif name == "bh":
            spread.eight_middle(slots8)
        elif name == "bi":
            spread.eight_end(slots8)
        elif name == "w":
            leave(layer, (raw_whole, through)[layer])
        elif name == "bn":
            add_gains(layer)
    scatter.end()
    settle()
    for place, copy in enumerate(leaving):
        copy.wait_recv() if place % 2 else copy.wait()
    hops.drain()


def both_layers(packs, raw, tables, owners):
    count = lax.axis_size("dp")
    kinds = count // 2
    anywhere = pl.BlockSpec(memory_space=pl.ANY)
    inside = pl.BlockSpec(memory_space=pltpu.VMEM)
    seqs, length = owners.shape
    tokens = seqs * length
    here, width = tokens // 4, packs[0].shape[-2] * count
    rows = width // count
    columns = [pack.shape[-1] for pack in packs]
    head_width = columns[OUT]
    heads = head_width // HEAD_SIZE
    group = 2 * width // count
    shape = lambda *dims: jax.ShapeDtypeStruct(dims, BF16)
    ends = [shape(*raw[0].shape)] * 2
    sums = [shape(*((2, 2) if IS_SHARED[a] else (2,)), rows, columns[a]) for a in range(4)]
    full = [shape(width, columns[a]) for a in range(4)] * 2
    rest = (
        [shape(4, here, width)] * 2
        + [shape(8 * here, columns[DOWN])] * 2
        + [shape(8, here, width), shape(8 * here, columns[GU]), shape(8, here, width)]
    )
    blocks = [shape(kinds, rows, columns[a]) for a in range(4)] * 6
    far = ends + sums + [shape(*pack.shape[1:]) for pack in packs] + full + rest + blocks
    near = [jax.ShapeDtypeStruct((1, width), F32)] * 2
    inner = lambda *dims: pltpu.VMEM(dims, BF16)
    block = lambda *lead: pltpu.VMEM(lead + (here, width), BF16)
    wide = pltpu.VMEM((here, width), F32)
    wires = 2 * 8 * count + 8 * kinds + 6 * (12 + width // group) + 80
    scratch = [
        pltpu.SemaphoreType.DMA((wires,)),
        pltpu.SemaphoreType.DMA((wires,)),
        pltpu.SemaphoreType.DMA((8 * kinds + 60,)),
        inner(width, columns[DOWN]),
        inner(width, columns[OUT]),
        inner(width, columns[GU]),
        block(4),
        block(8),
        block(8),
        block(8),
        pltpu.VMEM((columns[QKV], tokens), F32),
        inner(8 * here, columns[GU]),
        inner(8 * here, columns[DOWN]),
    ]
    scratch += [inner(columns[QKV], tokens)] * 2 + [inner(tokens, head_width)] * 2
    scratch += [pltpu.VMEM((heads, tokens), F32)] * 2 + [wide] * 2
    scratch += [inner(head_width, length), inner(tokens, columns[QKV])]
    scratch += [inner(kinds, rows, columns[a]) for a in range(4)] + [inner(rows, max(columns))]
    scratch += [wide] * 3 + [block()] * 3
    sums_of = count.bit_length() + 1
    scratch += [
        pltpu.VMEM((2, 2, 1, width), F32),
        pltpu.VMEM((4, width), F32),
        pltpu.VMEM((sums_of + 1, 4, width), F32),
        pltpu.VMEM((sums_of, 4, width), F32),
    ]
    part = inner(here // 2, width)
    scratch += [block(), block(), block(4), block(3), block(), block(), part, part, block(), part]
    results = pl.pallas_call(
        functools.partial(layers_kernel, count, heads, group),
        out_shape=far + near,
        in_specs=[anywhere] * 8 + [inside] * 4,
        out_specs=[anywhere] * len(far) + [inside] * 2,
        scratch_shapes=scratch,
        compiler_params=pltpu.CompilerParams(
            collective_id=0, has_side_effects=True, vmem_limit_bytes=62 * 1024 * 1024
        ),
    )(*packs, *raw, *tables, owners[:, :, None], owners[:, None, :])
    return results[:2], results[2:6], results[-2:]


def unit_tiles(units, section, shared):
    tiles = units // 256
    first = section * units // 128 + shared * tiles
    return [(first + j) * 128 for j in range(tiles)], section * units + 256 * tiles + shared * 64


def pack_kernel(w_query, keyval, w_out, w_gate_up, w_down, qkv, out, gate_up, down):
    half = qkv.shape[2] - 2 * HEAD_SIZE
    units = w_down.shape[2] // 2
    for section in range(2):
        at = slice(section * half, (section + 1) * half)
        place = slice(section * HEAD_SIZE, (section + 1) * HEAD_SIZE)
        qkv[section, :, :half] = w_query[0, :, at]
        qkv[section, :, half:] = jnp.concatenate([keyval[0, :, 0, place], keyval[0, :, 1, place]], 1)
        out[section] = w_out[0, :, at]
        for shared in range(2):
            tiles, tail = unit_tiles(units, section, shared)
            for j, first in enumerate(tiles):
                for kind in range(2):
                    at = slice(256 * j + 128 * kind, 256 * j + 128 * kind + 128)
                    gate_up[section, shared, :, at] = w_gate_up[0, :, kind, first : first + 128]
                down[section, shared, :, 128 * j : 128 * j + 128] = w_down[0, :, first : first + 128]
            end = slice(tail, tail + 64)
            gate_up[section, shared, :, 256 * len(tiles) :] = jnp.concatenate(
                [w_gate_up[0, :, 0, end], w_gate_up[0, :, 1, end]], 1
            )
            some = w_down[0, :, end]
            down[section, shared, :, 128 * len(tiles) :] = jnp.concatenate(
                [some, jnp.zeros_like(some)], 1
            )


def unpack_kernel(qkv, out, gate_up, down, w_query, keyval, w_out, w_gate_up, w_down):
    half = qkv.shape[2] - 2 * HEAD_SIZE
    units = w_down.shape[2] // 2
    for section in range(2):
        at = slice(section * half, (section + 1) * half)
        w_query[0, :, at] = qkv[section, :, :half].astype(F32)
        w_out[0, :, at] = out[section].astype(F32)
        for shared in range(2):
            tiles, tail = unit_tiles(units, section, shared)
            for j, first in enumerate(tiles):
                for kind in range(2):
                    at = slice(256 * j + 128 * kind, 256 * j + 128 * kind + 128)
                    w_gate_up[0, :, kind, first : first + 128] = gate_up[section, shared, :, at].astype(F32)
                w_down[0, :, first : first + 128] = down[section, shared, :, 128 * j : 128 * j + 128].astype(F32)
        tiles, tail = unit_tiles(units, section, 0)
        last = slice(256 * len(tiles), 256 * len(tiles) + 128)
        both = [gate_up[section, shared, :, last].astype(F32) for shared in range(2)]
        w_gate_up[0, :, 0, tail : tail + 128] = jnp.concatenate([both[0][:, :64], both[1][:, :64]], 1)
        w_gate_up[0, :, 1, tail : tail + 128] = jnp.concatenate([both[0][:, 64:], both[1][:, 64:]], 1)
        at = slice(128 * len(tiles), 128 * len(tiles) + 64)
        w_down[0, :, tail : tail + 128] = jnp.concatenate(
            [down[section, shared, :, at].astype(F32) for shared in range(2)], 1
        )
    for kind in range(2):
        start = half + kind * HEAD_SIZE
        keyval[0, :, kind, :] = jnp.concatenate(
            [qkv[section, :, start : start + HEAD_SIZE].astype(F32) for section in range(2)], 1
        )


def row_specs(shapes, step):
    specs = []
    for dims, axis in shapes:
        block = tuple(step if i == axis else size for i, size in enumerate(dims))
        specs.append(
            pl.BlockSpec(block, functools.partial(lambda n, a, i: tuple(i if k == a else 0 for k in range(n)), len(dims), axis))
        )
    return specs


def packed(raw, kernel, outs, raw_first):
    rows = raw[0].shape[1] if raw_first else raw[0].shape[-2]
    step = min(rows, 32 if raw_first else 128)
    wide = [(block.shape, 1) for block in (raw if raw_first else outs)]
    narrow = [(block.shape, len(block.shape) - 2) for block in (outs if raw_first else raw)]
    first, second = row_specs(wide, step), row_specs(narrow, step)
    return pl.pallas_call(
        kernel,
        grid=(rows // step,),
        out_shape=outs,
        in_specs=first if raw_first else second,
        out_specs=second if raw_first else first,
        compiler_params=pltpu.CompilerParams(vmem_limit_bytes=62 * 1024 * 1024),
    )(*raw)


def shards(
    layer_in,
    out_grad,
    doc_lengths,
    attn_gain,
    w_query,
    keyval_weight,
    w_out,
    mlp_gain,
    w_gate_up,
    w_down,
):
    micro, seqs, here, columns = layer_in.shape
    length = here * lax.axis_size("tensor")
    rows = w_query.shape[1]
    head_width = w_query.shape[2] // 2
    units = w_down.shape[2] // 4
    shape = jax.ShapeDtypeStruct
    raw = [w_query, keyval_weight, w_out, w_gate_up, w_down]
    packs = packed(
        raw,
        pack_kernel,
        [
            shape((2, rows, head_width + 2 * HEAD_SIZE), BF16),
            shape((2, rows, head_width), BF16),
            shape((2, 2, rows, 2 * units), BF16),
            shape((2, 2, rows, units + -units % 128), BF16),
        ],
        True,
    )
    owners = owners_of(doc_lengths.reshape(micro * seqs, -1), length)
    tables = rope_tables(length)
    (layer_out, in_grad), sums, (attn_term, mlp_term) = both_layers(
        packs, [layer_in, out_grad, attn_gain, mlp_gain], tables, owners
    )
    grads = packed(sums, unpack_kernel, [shape(block.shape, F32) for block in raw], False)
    grad_q, grad_kv, grad_o, grad_gu, grad_d = grads
    return layer_out, in_grad, attn_term, grad_q, grad_kv, grad_o, mlp_term, grad_gu, grad_d


def solution(mesh):
    activation = P(None, "dp", "tensor", "section")
    matrix = P("section", "dp", "tensor")
    stacked = P("section", "dp", None, "tensor")
    gain = P("section", None)
    return jax.shard_map(
        shards,
        mesh=mesh,
        in_specs=(
            activation,
            activation,
            P(None, "dp", None),
            gain,
            matrix,
            stacked,
            matrix,
            gain,
            stacked,
            matrix,
        ),
        out_specs=(
            activation,
            activation,
            gain,
            matrix,
            stacked,
            matrix,
            gain,
            stacked,
            matrix,
        ),
        check_vma=False,
    )
```
